32 devices in a mesh: rep: 8 (over z, x), par: 4 (over y, core).
Axes of the slice: x: 2, y: 2, z: 4, core: 2. Of those that a mesh axis runs over, the one named last changes fastest.
Arguments:
- activations: bfloat16 [2, 16384, 8192], P(None, 'rep', 'par'), may hold values from -12 to 12, as said below
- output_grads: bfloat16 [2, 16384, 1024], P(None, 'rep'), may hold values from -12 to 12, as said below
Outputs:
- combined: bfloat16 [2, 8192, 1024], P(None, ('par', 'rep'))
The draws below stay inside these ranges and needn't reach their ends.
Inputs may be any that keep to these rules, and one draw needn't show every extreme that they name: `activations`: activations of one replica and layer. `output_grads`: output gradients of one replica and layer.
All inputs are finite; a program needn't handle non-finite values.
Results may differ from the reference program's by a relative error of at most 0.0062.
Values may be sent and summed in bfloat16 or wider, within the bound.
No kernel may reach another device: no remote copies, remote signals or barrier semaphores. Data moves between devices by JAX's collectives and lax.ppermute only.
A program may use at most 128 MiB of HBM per device.

```python
import jax
import jax.numpy as jnp
from jax import lax

D = 8192
KV = 1024
LAYERS = 2
TOK_DEV = 2048
REPLICAS = 8
TOKENS = 16384


def column_profile(key, width, rising):
    rough = jnp.exp(jax.random.uniform(key, (width,), jnp.float32, -0.6, 0.6))
    position = jnp.arange(width).astype(jnp.float32) / width - 0.5
    return rough * jnp.exp(rising * jnp.log(3.0) * position)


def mixed_draw(key, width):
    common = jax.random.normal(jax.random.fold_in(key, 11), (LAYERS, TOK_DEV, width), jnp.float32)
    own = jax.random.normal(jax.random.fold_in(key, 12), (LAYERS, TOKENS, width), jnp.float32)
    replica_ids = (jnp.arange(TOKENS) // TOK_DEV).astype(jnp.float32)
    jitter = jnp.exp(jax.random.uniform(jax.random.fold_in(key, 13), (REPLICAS,), jnp.float32, -0.2, 0.2))
    own_weight = 0.5 * jnp.exp(jnp.log(3.0) * replica_ids / (REPLICAS - 1)) * jnp.repeat(jitter, TOK_DEV)
    columns_common = column_profile(jax.random.fold_in(key, 14), width, 1.0)
    columns_own = column_profile(jax.random.fold_in(key, 15), width, -1.0)
    shared_part = jnp.tile(common * columns_common[None, None, :], (1, REPLICAS, 1))
    own_part = own_weight[None, :, None] * own * columns_own[None, None, :]
    whole = (shared_part + own_part) * TOK_DEV ** (-0.25) * 0.5
    return jnp.clip(whole, -12.0, 12.0)


def draw_activations(key, part):
    return mixed_draw(jax.random.fold_in(key, 1), D).astype(jnp.bfloat16)


def draw_output_grads(key, part):
    return mixed_draw(jax.random.fold_in(key, 2), KV).astype(jnp.bfloat16)


def setup_inputs(seed: int = 0) -> dict:
    keys = jax.random.split(jax.random.key(seed), 3)
    activations = draw_activations(jax.random.fold_in(keys[2], 71), 0)
    output_grads = draw_output_grads(jax.random.fold_in(keys[2], 71), 0)
    return {"activations": activations, "output_grads": output_grads}


epsilon = 1e-6


def adasum_pair(first_part, second_part):
    first_wide = first_part.astype(jnp.float32)
    second_wide = second_part.astype(jnp.float32)
    dot_value = jnp.sum(first_wide * second_wide)
    norm_first = jnp.sum(first_wide * first_wide)
    norm_second = jnp.sum(second_wide * second_wide)
    result = (1.0 - dot_value / (2.0 * (norm_first + epsilon))) * first_wide
    result = result + (1.0 - dot_value / (2.0 * (norm_second + epsilon))) * second_wide
    return result.astype(jnp.bfloat16)


def one_replica(pair):
    return jnp.dot(pair[0].T, pair[1], preferred_element_type=jnp.float32).astype(jnp.bfloat16)


def reference(activations, output_grads):
    results = []
    for layer_index in range(LAYERS):
        inputs_rep = activations[layer_index].reshape(REPLICAS, TOK_DEV, D)
        grads_rep = output_grads[layer_index].reshape(REPLICAS, TOK_DEV, KV)
        gradients = lax.map(one_replica, (inputs_rep, grads_rep))
        while gradients.shape[0] > 1:
            gradients = jax.vmap(adasum_pair)(gradients[0::2], gradients[1::2])
        results.append(gradients[0])
    return jnp.stack(results)
```

```python
import functools

import jax
import jax.numpy as jnp
from jax import lax
from jax.experimental import pallas as pl
from jax.experimental.pallas import tpu as pltpu
from jax.sharding import PartitionSpec as P

epsilon = 1e-06
VMEM_LIMIT = 50 * 1024 * 1024
LANES = 128


def exchange(value, axis, mask):
    return lax.ppermute(value, axis, [(i, i ^ mask) for i in range(lax.axis_size(axis))])


def gradient_blocks(activations, output_grads, layer, blocks, rows):
    tokens, width_out = output_grads.shape[1:]
    count = len(blocks)
    depth = min(512, tokens)
    steps = tokens // depth
    wide_rows = max(rows, LANES)
    shared = wide_rows // rows

    def kernel(ids, a_ref, b_ref, *refs):
        outs, total = refs[:count], refs[count]
        unit, step = pl.program_id(0), pl.program_id(1)
        part = lax.dot_general(
            a_ref[0],
            b_ref[0, pl.ds(pl.multiple_of(step * depth, depth), depth), :],
            (((0,), (0,)), ((), ())),
            preferred_element_type=jnp.float32,
        )

        @pl.when(step == 0)
        def _():
            total[...] = part

        @pl.when(step > 0)
        def _():
            total[...] += part

        for index in range(count):

            @pl.when((unit == index) & (step == steps - 1))
            def _(index=index):
                first = pl.multiple_of(lax.rem(ids[unit], shared) * rows, rows)
                outs[index][...] = total[pl.ds(first, rows), :].astype(jnp.bfloat16)

    shape = jax.ShapeDtypeStruct((rows, width_out), jnp.bfloat16)
    return pl.pallas_call(
        kernel,
        grid_spec=pltpu.PrefetchScalarGridSpec(
            num_scalar_prefetch=1,
            grid=(count, steps),
            in_specs=[
                pl.BlockSpec((1, depth, wide_rows), lambda u, k, ids: (layer, k, ids[u] // shared)),
                pl.BlockSpec((1, tokens, width_out), lambda u, k, ids: (layer, 0, 0)),
            ],
            out_specs=[pl.BlockSpec((rows, width_out), lambda u, k, ids: (0, 0))] * count,
            scratch_shapes=[pltpu.VMEM((wide_rows, width_out), jnp.float32)],
        ),
        out_shape=[shape] * count,
        compiler_params=pltpu.CompilerParams(vmem_limit_bytes=VMEM_LIMIT),
        cost_estimate=pl.CostEstimate(
            flops=2 * count * tokens * rows * width_out,
            bytes_accessed=2 * (tokens * width_out + count * rows * (tokens + width_out)),
            transcendentals=0,
        ),
        name="gradient_blocks",
    )(jnp.stack(blocks), activations, output_grads)


def pair_row(first, second, count):
    low, high = jnp.minimum(first, second), jnp.maximum(first, second)
    return low * (2 * count - 1 - low) // 2 + high


def gram_rows(rank, parts):
    count = len(parts)
    rows, width = parts[0].shape
    pairs = [(u, v) for u in range(count) for v in range(u, count)]
    padded = -(-len(pairs) // 8) * 8
    stride = 16

    def kernel(rank_ref, *refs):
        ins, out = refs[:count], refs[count]

        def body(index, totals):
            where = pl.ds(pl.multiple_of(index * stride, stride), stride)
            totals = list(totals)
            for column in range(0, width, LANES):
                wide = [ref[where, column : column + LANES].astype(jnp.float32) for ref in ins]
                for number, (u, v) in enumerate(pairs):
                    product = wide[u] * wide[v]
                    totals[number] = totals[number] + (product[:8] + product[8:])
            return tuple(totals)

        zero = jnp.zeros((8, LANES), jnp.float32)
        totals = lax.fori_loop(0, rows // stride, body, (zero,) * len(pairs))
        out[...] = jnp.zeros_like(out)
        mine = rank_ref[0]
        for number, (u, v) in enumerate(pairs):
            row = pair_row(mine ^ u, mine ^ v, count)
            out[pl.ds(row, 1), :] = jnp.sum(totals[number], axis=0, keepdims=True)

    return pl.pallas_call(
        kernel,
        in_specs=[pl.BlockSpec(memory_space=pltpu.SMEM)]
        + [pl.BlockSpec(memory_space=pltpu.VMEM)] * count,
        out_specs=pl.BlockSpec(memory_space=pltpu.VMEM),
        out_shape=jax.ShapeDtypeStruct((padded, LANES), jnp.float32),
        compiler_params=pltpu.CompilerParams(vmem_limit_bytes=VMEM_LIMIT),
        cost_estimate=pl.CostEstimate(
            flops=2 * len(pairs) * rows * width,
            bytes_accessed=2 * count * rows * width,
            transcendentals=0,
        ),
        name="gram_rows",
    )(rank, *parts)


def tree_weights(gram, count):
    factors = [1.0] * count
    scales = []
    size = 1
    while size < count:
        level = []
        for start in range(0, count, 2 * size):
            first = range(start, start + size)
            second = range(start + size, start + 2 * size)

            def form(left, right):
                terms = [factors[i] * factors[j] * gram(i, j) for i in left for j in right]
                return functools.reduce(lambda a, b: a + b, terms)

            dot_value = form(first, second)
            norm_first = jnp.maximum(form(first, first), 0.0)
            norm_second = jnp.maximum(form(second, second), 0.0)
            first_scale = 1.0 - dot_value / (2.0 * (norm_first + epsilon))
            second_scale = 1.0 - dot_value / (2.0 * (norm_second + epsilon))
            level += [first_scale, second_scale]
            for i in first:
                factors[i] = factors[i] * first_scale
            for i in second:
                factors[i] = factors[i] * second_scale
        scales.append(level)
        size *= 2
    return scales


def combine(rank, grams, layer_parts):
    layers, count = len(layer_parts), len(layer_parts[0])
    rows, width = layer_parts[0][0].shape
    levels = count.bit_length() - 1
    stride = 16

    def kernel(rank_ref, gram_ref, *refs):
        out = refs[layers * count]
        mine = rank_ref[0]
        padded = gram_ref.shape[0] // layers
        sums = jnp.sum(gram_ref[...], axis=1, keepdims=True)
        for layer in range(layers):
            ins = refs[layer * count : (layer + 1) * count]

            def gram(i, j):
                low, high = min(i, j), max(i, j)
                row = layer * padded + low * (2 * count - 1 - low) // 2 + high
                return sums[row : row + 1]

            scales = tree_weights(gram, count)
            relative = []
            for level, values in enumerate(scales):
                group = mine >> level
                moved = list(values)
                for bit in range(levels - level):
                    flip = ((group >> bit) & 1) == 1
                    moved = [
                        jnp.where(flip, moved[i ^ (1 << bit)], moved[i]) for i in range(len(moved))
                    ]
                relative.append([jnp.broadcast_to(value, (stride, LANES)) for value in moved])

            def body(index, carry):
                where = pl.ds(pl.multiple_of(index * stride, stride), stride)
                for column in range(0, width, LANES):
                    held = [ref[where, column : column + LANES] for ref in ins]
                    for level in range(levels):
                        wide = [value.astype(jnp.float32) for value in held]
                        held = [
                            (
                                relative[level][2 * pair] * wide[2 * pair]
                                + relative[level][2 * pair + 1] * wide[2 * pair + 1]
                            ).astype(jnp.bfloat16)
                            for pair in range(len(held) // 2)
                        ]
                    out[layer, where, column : column + LANES] = held[0]
                return carry

            lax.fori_loop(0, rows // stride, body, 0)

    return pl.pallas_call(
        kernel,
        in_specs=[pl.BlockSpec(memory_space=pltpu.SMEM)]
        + [pl.BlockSpec(memory_space=pltpu.VMEM)] * (1 + layers * count),
        out_specs=pl.BlockSpec(memory_space=pltpu.VMEM),
        out_shape=jax.ShapeDtypeStruct((layers, rows, width), jnp.bfloat16),
        compiler_params=pltpu.CompilerParams(vmem_limit_bytes=VMEM_LIMIT),
        cost_estimate=pl.CostEstimate(
            flops=3 * layers * count * rows * width,
            bytes_accessed=2 * layers * (count + 1) * rows * width,
            transcendentals=0,
        ),
        name="combine",
    )(rank, grams, *[part for parts in layer_parts for part in parts])


def level_masks(levels):
    masks = [1 << level for level in range(levels)]
    if levels >= 3:
        masks[-1] |= masks[-2]
    return masks


def spread(code, masks):
    value = 0
    for bit, mask in enumerate(masks):
        if code >> bit & 1:
            value ^= mask
    return value


def transfer_rounds(levels, layers):
    count = 1 << levels
    queues = []
    for level in range(levels):
        units = []
        for block in range(count):
            if block & ((2 << level) - 1) == 1 << level:
                for part in range(1 << level):
                    units.append((block, part))
        queues.append(units)
    arrival = {}
    rounds = []
    for slot in range(count // 2):
        chosen = []
        for level in range(levels):

            def ready(unit):
                block, part = unit
                if part == 0:
                    return -1
                top = part.bit_length() - 1
                return arrival.get((top, block | 1 << top, part ^ 1 << top), count)

            able = [unit for unit in queues[level] if ready(unit) < slot]
            able.sort(key=lambda unit: (-(unit[0] >> (level + 1)), -unit[1]))
            unit = able[0]
            queues[level].remove(unit)
            chosen.append(unit)
        for level, unit in enumerate(chosen):
            arrival[(level,) + unit] = slot
        rounds += [[(layer,) + unit for unit in chosen] for layer in range(layers)]
    return rounds


def body(activations, output_grads):
    replicas = lax.axis_size("rep")
    levels = replicas.bit_length() - 1
    layers, _, width = activations.shape
    rows = width // replicas
    rank = lax.axis_index("rep")
    masks = level_masks(levels)
    rounds = transfer_rounds(levels, layers)

    held = {}

    def make(layer, codes):
        blocks = [rank ^ spread(code, masks) for code in codes]
        for code, value in zip(codes, gradient_blocks(activations, output_grads, layer, blocks, rows)):
            held[layer, code, 0] = value

    wanted = [[] for _ in range(layers)]
    for chosen in rounds:
        for level, (layer, block, part) in enumerate(chosen):
            for code in (block,):
                if part == 0 and code not in wanted[layer]:
                    wanted[layer].append(code)
    wanted = [codes + [0] for codes in wanted]
    early = [[chosen[level][1] for level in range(levels)] for chosen in rounds[:layers]]
    for layer in range(layers):
        make(layer, early[layer])
    for layer in range(layers):
        make(layer, [code for code in wanted[layer] if code not in early[layer]])

    in_flight = []
    for chosen in rounds:
        sent = [held[unit] for unit in chosen]
        if len(in_flight) >= layers:
            keys = in_flight.pop(0)
            joined = lax.optimization_barrier(tuple(sent) + tuple(held[key] for key in keys))
            sent = joined[: len(sent)]
            for key, value in zip(keys, joined[len(sent) :]):
                held[key] = value
        keys = []
        for level, (layer, block, part) in enumerate(chosen):
            key = (layer, block ^ 1 << level, part | 1 << level)
            held[key] = exchange(sent[level], "rep", masks[level])
            keys.append(key)
        in_flight.append(keys)

    order = {spread(code, masks): code for code in range(replicas)}
    parts = [[held[layer, 0, order[step]] for step in range(replicas)] for layer in range(layers)]
    position = jnp.reshape(rank, (1,)).astype(jnp.int32)
    grams = jnp.concatenate([gram_rows(position, parts[layer]) for layer in range(layers)])
    par = lax.axis_size("par")
    stride = 1
    while stride < par:
        grams = grams + exchange(grams, "par", stride)
        stride *= 2
    for mask in masks:
        grams = grams + exchange(grams, "rep", mask)
    return combine(position, grams, parts)


def solution(mesh):
    return jax.shard_map(
        body,
        mesh=mesh,
        in_specs=(P(None, "rep", "par"), P(None, "rep", None)),
        out_specs=P(None, ("par", "rep"), None),
        check_vma=False,
    )
```

```python
import jax
import jax.numpy as jnp
from jax import lax
from jax.experimental import pallas as pl
from jax.experimental.pallas import tpu as pltpu
from jax.sharding import PartitionSpec as P

epsilon = 1e-06
VMEM_LIMIT = 40 * 1024 * 1024
LANES = 128
STRIDE = 16
GROUP = 4
GRAM_ROWS = 16


def exchange(value, axis, mask):
    return lax.ppermute(value, axis, [(i, i ^ mask) for i in range(lax.axis_size(axis))])


def tied(values, others):
    joined = lax.optimization_barrier(tuple(values) + tuple(others))
    return list(joined[: len(values)]), list(joined[len(values) :])


def call(kernel, name, rank, inputs, outputs, flops):
    size = sum(x.size * x.dtype.itemsize for x in list(inputs) + list(outputs))
    return pl.pallas_call(
        kernel,
        in_specs=[pl.BlockSpec(memory_space=pltpu.SMEM)]
        + [pl.BlockSpec(memory_space=pltpu.VMEM)] * len(inputs),
        out_specs=[pl.BlockSpec(memory_space=pltpu.VMEM)] * len(outputs),
        out_shape=list(outputs),
        compiler_params=pltpu.CompilerParams(vmem_limit_bytes=VMEM_LIMIT),
        cost_estimate=pl.CostEstimate(flops=flops, bytes_accessed=size, transcendentals=0),
        name=name,
    )(rank, *inputs)


def pair_row(first, second):
    low, high = jnp.minimum(first, second), jnp.maximum(first, second)
    return low * (2 * GROUP - 1 - low) // 2 + high


def tiles(rows, width, step, start):
    def body(index, carry):
        where = pl.ds(pl.multiple_of(index * STRIDE, STRIDE), STRIDE)
        for column in range(0, width, LANES):
            carry = step(where, slice(column, column + LANES), carry)
        return carry

    return lax.fori_loop(0, rows // STRIDE, body, start)


def gram_rows(rank, parts, before):
    rows, width = parts[0].shape
    pairs = [(u, v) for u in range(GROUP) for v in range(u, GROUP)]

    def kernel(rank_ref, *refs):
        ins, old, out = refs[:GROUP], refs[GROUP], refs[GROUP + 1]

        def step(where, columns, totals):
            wide = [ref[where, columns].astype(jnp.float32) for ref in ins]
            new = []
            for total, (u, v) in zip(totals, pairs):
                product = wide[u] * wide[v]
                new.append(total + (product[:8] + product[8:]))
            return tuple(new)

        zero = jnp.zeros((8, LANES), jnp.float32)
        totals = tiles(rows, width, step, (zero,) * len(pairs))
        out[...] = old[...]
        mine = rank_ref[0] & (GROUP - 1)
        for total, (u, v) in zip(totals, pairs):
            row = pl.ds(pair_row(mine ^ u, mine ^ v), 1)
            out[row, :] = out[row, :] + jnp.sum(total, axis=0, keepdims=True)

    shape = jax.ShapeDtypeStruct((GRAM_ROWS, LANES), jnp.float32)
    flops = 2 * len(pairs) * rows * width
    return call(kernel, "gram_rows", rank, list(parts) + [before], [shape], flops)[0]


def scale_pair(dot_value, norm_first, norm_second):
    return (
        1.0 - dot_value / (2.0 * (norm_first + epsilon)),
        1.0 - dot_value / (2.0 * (norm_second + epsilon)),
    )


def weighted(first_scale, first_part, second_scale, second_part):
    result = first_scale * first_part.astype(jnp.float32)
    result = result + second_scale * second_part.astype(jnp.float32)
    return result.astype(jnp.bfloat16)


def group_combine(rank, gram, block_parts):
    rows, width = block_parts[0][0].shape

    def kernel(rank_ref, gram_ref, *refs):
        ins, outs = refs[: GROUP * len(block_parts)], refs[GROUP * len(block_parts) :]
        sums = jnp.sum(gram_ref[...], axis=1, keepdims=True)

        def entry(i, j):
            low, high = min(i, j), max(i, j)
            row = low * (2 * GROUP - 1 - low) // 2 + high
            return sums[row : row + 1]

        def norm(i, j, left, right):
            value = left * left * entry(i, i) + right * right * entry(j, j)
            return jnp.maximum(value + 2.0 * (left * right * entry(i, j)), 0.0)

        low_first, low_second = scale_pair(entry(0, 1), entry(0, 0), entry(1, 1))
        high_first, high_second = scale_pair(entry(2, 3), entry(2, 2), entry(3, 3))
        dot_value = (
            low_first * high_first * entry(0, 2)
            + low_first * high_second * entry(0, 3)
            + low_second * high_first * entry(1, 2)
            + low_second * high_second * entry(1, 3)
        )
        norm_low = norm(0, 1, low_first, low_second)
        norm_high = norm(2, 3, high_first, high_second)
        top_first, top_second = scale_pair(dot_value, norm_low, norm_high)

        odd = (rank_ref[0] & 1) == 1
        upper = (rank_ref[0] & 2) == 2
        low_first, low_second = (
            jnp.where(odd, low_second, low_first),
            jnp.where(odd, low_first, low_second),
        )
        high_first, high_second = (
            jnp.where(odd, high_second, high_first),
            jnp.where(odd, high_first, high_second),
        )
        scales = [
            jnp.where(upper, high_first, low_first),
            jnp.where(upper, high_second, low_second),
            jnp.where(upper, low_first, high_first),
            jnp.where(upper, low_second, high_second),
            jnp.where(upper, top_second, top_first),
            jnp.where(upper, top_first, top_second),
        ]
        scales = [jnp.broadcast_to(scale, (STRIDE, LANES)) for scale in scales]

        for number, out in enumerate(outs):
            block = ins[GROUP * number : GROUP * (number + 1)]

            def step(where, columns, carry, out=out, block=block):
                held = [ref[where, columns] for ref in block]
                near = weighted(scales[0], held[0], scales[1], held[1])
                far = weighted(scales[2], held[2], scales[3], held[3])
                out[where, columns] = weighted(scales[4], near, scales[5], far)
                return carry

            tiles(rows, width, step, 0)

    shape = jax.ShapeDtypeStruct((rows, width), jnp.bfloat16)
    inputs = [gram] + [part for parts in block_parts for part in parts]
    flops = 9 * len(block_parts) * rows * width
    return call(kernel, "group_combine", rank, inputs, [shape] * len(block_parts), flops)


def pair_rows(rank, kept, received, level, layer, before):
    rows, width = kept[0].shape

    def kernel(rank_ref, *refs):
        count = len(kept)
        mine, theirs, old, out = refs[:count], refs[count : 2 * count], refs[-2], refs[-1]
        totals = (jnp.zeros((8, LANES), jnp.float32),) * 3
        for left, right in zip(mine, theirs):

            def step(where, columns, totals, left=left, right=right):
                a, b = left[where, columns].astype(jnp.float32), right[where, columns].astype(jnp.float32)
                new = [
                    total + (product[:8] + product[8:])
                    for total, product in zip(totals, (a * b, a * a, b * b))
                ]
                return tuple(new)

            totals = tiles(rows, width, step, totals)
        upper = ((rank_ref[0] >> level) & 1) == 1
        dot_value, norm_mine, norm_theirs = [jnp.sum(t, axis=0, keepdims=True) for t in totals]
        out[...] = old[...]
        base = 3 * layer
        out[base : base + 1, :] = dot_value
        out[base + 1 : base + 2, :] = jnp.where(upper, norm_theirs, norm_mine)
        out[base + 2 : base + 3, :] = jnp.where(upper, norm_mine, norm_theirs)

    shape = jax.ShapeDtypeStruct(before.shape, jnp.float32)
    inputs = list(kept) + list(received) + [before]
    flops = 6 * len(kept) * rows * width
    return call(kernel, "pair_rows", rank, inputs, [shape], flops)[0]


def pair_combine(rank, sums, kept, received, level):
    layers, count = len(kept), len(kept[0])
    rows, width = kept[0][0].shape

    def kernel(rank_ref, sums_ref, *refs):
        ins, outs = refs[: 2 * layers * count], refs[2 * layers * count :]
        totals = jnp.sum(sums_ref[...], axis=1, keepdims=True)
        upper = ((rank_ref[0] >> level) & 1) == 1
        for layer in range(layers):
            dot_value, norm_first, norm_second = [
                totals[3 * layer + k : 3 * layer + k + 1] for k in range(3)
            ]
            first, second = scale_pair(dot_value, norm_first, norm_second)
            mine = jnp.broadcast_to(jnp.where(upper, second, first), (STRIDE, LANES))
            theirs = jnp.broadcast_to(jnp.where(upper, first, second), (STRIDE, LANES))
            for number in range(count):
                left, right = ins[2 * (layer * count + number) :][:2]
                out = outs[number]

                def step(where, columns, carry, left=left, right=right, out=out):
                    out[layer, where, columns] = weighted(
                        mine, left[where, columns], theirs, right[where, columns]
                    )
                    return carry

                tiles(rows, width, step, 0)

    shape = jax.ShapeDtypeStruct((layers, rows, width), jnp.bfloat16)
    inputs = [sums]
    for layer in range(layers):
        for left, right in zip(kept[layer], received[layer]):
            inputs += [left, right]
    flops = 3 * layers * count * rows * width
    return call(kernel, "pair_combine", rank, inputs, [shape] * count, flops)


def level_masks(levels):
    masks = [1 << level for level in range(levels)]
    if levels >= 3:
        masks[-1] |= masks[-2]
    return masks


def spread(code, masks):
    value = 0
    for bit, mask in enumerate(masks):
        if code >> bit & 1:
            value ^= mask
    return value


def body(activations, output_grads):
    replicas = lax.axis_size("rep")
    par = lax.axis_size("par")
    levels = replicas.bit_length() - 1
    layers, tokens, width = activations.shape
    rows = width // replicas
    rank = lax.axis_index("rep")
    position = jnp.reshape(rank, (1,)).astype(jnp.int32)
    masks = level_masks(levels)
    tails = [tail << 2 for tail in reversed(range(replicas // GROUP))]

    def near_pair(layer, code):
        first = ((rank ^ spread(code, masks)) >> 1) * (2 * rows)
        columns = lax.dynamic_slice(activations, (layer, 0, first), (1, tokens, 2 * rows))[0]
        product = lax.dot_general(
            columns,
            output_grads[layer],
            (((0,), (0,)), ((), ())),
            preferred_element_type=jnp.float32,
        ).astype(jnp.bfloat16)
        side = (rank ^ spread(code, masks)) & 1
        return (
            lax.dynamic_slice_in_dim(product, side * rows, rows, 0),
            lax.dynamic_slice_in_dim(product, (1 - side) * rows, rows, 0),
        )

    own, crossed, far, far_crossed = {}, {}, {}, {}
    rounds = []
    for layer in range(layers):
        codes = [2 | tail for tail in tails] + tails
        second = [("own", 2 | tail) for tail in tails] + [("crossed", 2 | tail) for tail in tails]
        rounds += [(layer, code, unit) for code, unit in zip(codes, second)]

    grams = []
    flying = []

    def land():
        layer, code, unit = flying.pop(0)
        return layer, code, unit

    def settle(sends):
        layer, code, (kind, block) = flying.pop(0)
        target = far if kind == "own" else far_crossed
        key, other = (layer, code), (layer, block ^ 2)
        sends, (crossed[key], target[other]) = tied(sends, [crossed[key], target[other]])
        return sends

    sums = [jnp.zeros((GRAM_ROWS, LANES), jnp.float32) for _ in range(layers)]

    def gather(layer, tail):
        key = (layer, tail)
        parts = [own[key], crossed[key], far[key], far_crossed[key]]
        sums[layer] = gram_rows(position, parts, sums[layer])

    for layer, code, (kind, block) in rounds:
        own[layer, code], sent = near_pair(layer, code)
        passed = own[layer, block] if kind == "own" else crossed[layer, block]
        if len(flying) == 2:
            sent, passed = settle([sent, passed])
        crossed[layer, code] = exchange(sent, "rep", masks[0])
        target = far if kind == "own" else far_crossed
        target[layer, block ^ 2] = exchange(passed, "rep", masks[1])
        flying.append((layer, code, (kind, block)))

    spans = []
    stride = 1
    while stride < par:
        spans.append(("par", stride))
        stride *= 2

    for layer in range(layers):
        for tail in tails:
            gather(layer, tail)
    combined = []
    for layer in range(layers):
        last = layer == layers - 1
        near = [("rep", masks[0])]
        hops = [("rep", masks[1])] + spans + near if last else spans + near + [("rep", masks[1])]
        for axis, mask in hops:
            sums[layer] = sums[layer] + exchange(sums[layer], axis, mask)
        parts = [
            [held[layer, tail] for held in (own, crossed, far, far_crossed)] for tail in tails
        ]
        combined.append(dict(zip(tails, group_combine(position, sums[layer], parts))))

    for level in range(2, levels):
        keep = [tail for tail in tails if not tail >> level & 1 and tail in combined[0]]
        totals = jnp.zeros((-(-3 * layers // 8) * 8, LANES), jnp.float32)
        kept, received = [], []
        for layer in range(layers):
            kept.append([combined[layer][tail] for tail in keep])
            received.append(
                [
                    exchange(combined[layer][tail | 1 << level], "rep", masks[level])
                    for tail in keep
                ]
            )
            totals = pair_rows(position, kept[layer], received[layer], level, layer, totals)
        for axis, mask in spans + [("rep", mask) for mask in masks[: level + 1]]:
            totals = totals + exchange(totals, axis, mask)
        results = pair_combine(position, totals, kept, received, level)
        if level < levels - 1:
            combined = [
                {tail: result[layer] for tail, result in zip(keep, results)} for layer in range(layers)
            ]
    return results[0]


def solution(mesh):
    return jax.shard_map(
        body,
        mesh=mesh,
        in_specs=(P(None, "rep", "par"), P(None, "rep", None)),
        out_specs=P(None, ("par", "rep"), None),
        check_vma=False,
    )
```

```python
import jax
import jax.numpy as jnp
from jax import lax
from jax.experimental import pallas as pl
from jax.experimental.pallas import tpu as pltpu
from jax.sharding import PartitionSpec as P

epsilon = 1e-06
LARGE_LIMIT = 60 * 1024 * 1024
SMALL_LIMIT = 16 * 1024 * 1024
LANES = 128
STRIDE = 16
GROUP = 4
GRAM_ROWS = 16
COST = 1024
BLOCK_COST = 1_600_000_000
GRAM_COST = 3_200_000_000
CROSS_COST = 4_000_000_000


def exchange(value, axis, mask):
    return lax.ppermute(value, axis, [(i, i ^ mask) for i in range(lax.axis_size(axis))])


def tied(values, others):
    joined = lax.optimization_barrier(tuple(values) + tuple(others))
    return list(joined[: len(values)]), list(joined[len(values) :])


def call(kernel, name, rank, inputs, outputs, flops=COST):
    return pl.pallas_call(
        kernel,
        in_specs=[pl.BlockSpec(memory_space=pltpu.SMEM)]
        + [pl.BlockSpec(memory_space=pltpu.VMEM)] * len(inputs),
        out_specs=[pl.BlockSpec(memory_space=pltpu.VMEM)] * len(outputs),
        out_shape=list(outputs),
        compiler_params=pltpu.CompilerParams(vmem_limit_bytes=SMALL_LIMIT),
        cost_estimate=pl.CostEstimate(flops=flops, bytes_accessed=COST, transcendentals=0),
        name=name,
    )(rank, *inputs)


def block_pair(rank, activations, output_grads, layer, offset, rows):
    tokens, width_out = output_grads.shape[1:]
    columns = min(512, width_out)

    def kernel(rank_ref, a_ref, b_ref, kept, sent, product):
        product[...] = lax.dot_general(
            a_ref[0], b_ref[0], (((0,), (0,)), ((), ())), preferred_element_type=jnp.float32
        )
        side = (rank_ref[0] ^ offset) & 1
        kept[...] = product[pl.ds(pl.multiple_of(side * rows, rows), rows), :].astype(jnp.bfloat16)
        sent[...] = product[pl.ds(pl.multiple_of((1 - side) * rows, rows), rows), :].astype(jnp.bfloat16)

    shape = jax.ShapeDtypeStruct((rows, width_out), jnp.bfloat16)
    return pl.pallas_call(
        kernel,
        grid_spec=pltpu.PrefetchScalarGridSpec(
            num_scalar_prefetch=1,
            grid=(width_out // columns,),
            in_specs=[
                pl.BlockSpec((1, tokens, 2 * rows), lambda j, rank: (layer, 0, (rank[0] ^ offset) >> 1)),
                pl.BlockSpec((1, tokens, columns), lambda j, rank: (layer, 0, j)),
            ],
            out_specs=[pl.BlockSpec((rows, columns), lambda j, rank: (0, j))] * 2,
            scratch_shapes=[pltpu.VMEM((2 * rows, columns), jnp.float32)],
        ),
        out_shape=[shape, shape],
        compiler_params=pltpu.CompilerParams(vmem_limit_bytes=LARGE_LIMIT),
        cost_estimate=pl.CostEstimate(flops=BLOCK_COST, bytes_accessed=COST, transcendentals=0),
        name="block_pair",
    )(rank, activations, output_grads)


def pair_row(first, second):
    low, high = jnp.minimum(first, second), jnp.maximum(first, second)
    return low * (2 * GROUP - 1 - low) // 2 + high


def tiles(rows, width, step, start):
    def body(index, carry):
        where = pl.ds(pl.multiple_of(index * STRIDE, STRIDE), STRIDE)
        for column in range(0, width, LANES):
            carry = step(where, slice(column, column + LANES), carry)
        return carry

    return lax.fori_loop(0, rows // STRIDE, body, start)


def gram_rows(rank, parts, before, cost):
    rows, width = parts[0].shape
    pairs = [(u, v) for u in range(GROUP) for v in range(u, GROUP)]

    def kernel(rank_ref, *refs):
        ins, out = refs[:GROUP], refs[-1]

        def step(where, columns, totals):
            wide = [ref[where, columns].astype(jnp.float32) for ref in ins]
            new = []
            for total, (u, v) in zip(totals, pairs):
                product = wide[u] * wide[v]
                new.append(total + (product[:8] + product[8:]))
            return tuple(new)

        zero = jnp.zeros((8, LANES), jnp.float32)
        totals = tiles(rows, width, step, (zero,) * len(pairs))
        out[...] = jnp.zeros_like(out) if before is None else refs[GROUP][...]
        mine = rank_ref[0] & (GROUP - 1)
        for total, (u, v) in zip(totals, pairs):
            row = pl.ds(pair_row(mine ^ u, mine ^ v), 1)
            out[row, :] = out[row, :] + jnp.sum(total, axis=0, keepdims=True)

    shape = jax.ShapeDtypeStruct((GRAM_ROWS, LANES), jnp.float32)
    inputs = list(parts) + ([] if before is None else [before])
    return call(kernel, "gram_rows", rank, inputs, [shape], cost)[0]


def total(values, cost):
    def kernel(*refs):
        parts = [ref[...] for ref in refs[:-1]]
        while len(parts) > 1:
            parts = [left + right for left, right in zip(parts[::2], parts[1::2])]
        refs[-1][...] = parts[0]

    return pl.pallas_call(
        kernel,
        in_specs=[pl.BlockSpec(memory_space=pltpu.VMEM)] * len(values),
        out_specs=pl.BlockSpec(memory_space=pltpu.VMEM),
        out_shape=jax.ShapeDtypeStruct(values[0].shape, values[0].dtype),
        compiler_params=pltpu.CompilerParams(vmem_limit_bytes=SMALL_LIMIT),
        cost_estimate=pl.CostEstimate(flops=cost, bytes_accessed=COST, transcendentals=0),
        name="total",
    )(*values)


def scale_pair(dot_value, norm_first, norm_second):
    return (
        1.0 - dot_value / (2.0 * (norm_first + epsilon)),
        1.0 - dot_value / (2.0 * (norm_second + epsilon)),
    )


def weighted(first_scale, first_part, second_scale, second_part):
    result = first_scale * first_part.astype(jnp.float32)
    result = result + second_scale * second_part.astype(jnp.float32)
    return result.astype(jnp.bfloat16)


def group_combine(rank, gram, block_parts):
    rows, width = block_parts[0][0].shape

    def kernel(rank_ref, gram_ref, *refs):
        ins, outs = refs[: GROUP * len(block_parts)], refs[GROUP * len(block_parts) :]
        sums = jnp.sum(gram_ref[...], axis=1, keepdims=True)

        def entry(i, j):
            low, high = min(i, j), max(i, j)
            row = low * (2 * GROUP - 1 - low) // 2 + high
            return sums[row : row + 1]

        def norm(i, j, left, right):
            value = left * left * entry(i, i) + right * right * entry(j, j)
            return jnp.maximum(value + 2.0 * (left * right * entry(i, j)), 0.0)

        low_first, low_second = scale_pair(entry(0, 1), entry(0, 0), entry(1, 1))
        high_first, high_second = scale_pair(entry(2, 3), entry(2, 2), entry(3, 3))
        dot_value = (
            low_first * high_first * entry(0, 2)
            + low_first * high_second * entry(0, 3)
            + low_second * high_first * entry(1, 2)
            + low_second * high_second * entry(1, 3)
        )
        norm_low = norm(0, 1, low_first, low_second)
        norm_high = norm(2, 3, high_first, high_second)
        top_first, top_second = scale_pair(dot_value, norm_low, norm_high)

        odd = (rank_ref[0] & 1) == 1
        upper = (rank_ref[0] & 2) == 2
        low_first, low_second = (
            jnp.where(odd, low_second, low_first),
            jnp.where(odd, low_first, low_second),
        )
        high_first, high_second = (
            jnp.where(odd, high_second, high_first),
            jnp.where(odd, high_first, high_second),
        )
        scales = [
            jnp.where(upper, high_first, low_first),
            jnp.where(upper, high_second, low_second),
            jnp.where(upper, low_first, high_first),
            jnp.where(upper, low_second, high_second),
            jnp.where(upper, top_second, top_first),
            jnp.where(upper, top_first, top_second),
        ]
        scales = [jnp.broadcast_to(scale, (STRIDE, LANES)) for scale in scales]

        for number, out in enumerate(outs):
            block = ins[GROUP * number : GROUP * (number + 1)]

            def step(where, columns, carry, out=out, block=block):
                held = [ref[where, columns] for ref in block]
                near = weighted(scales[0], held[0], scales[1], held[1])
                far = weighted(scales[2], held[2], scales[3], held[3])
                out[where, columns] = weighted(scales[4], near, scales[5], far)
                return carry

            tiles(rows, width, step, 0)

    shape = jax.ShapeDtypeStruct((rows, width), jnp.bfloat16)
    inputs = [gram] + [part for parts in block_parts for part in parts]
    return call(kernel, "group_combine", rank, inputs, [shape] * len(block_parts))


def chosen_rows(rank_ref, level, candidates, where, columns):
    if len(candidates) == 1:
        return candidates[0][where, columns]
    middle = ((rank_ref[0] >> level) & 1) != ((rank_ref[0] >> (level - 1)) & 1)
    return jnp.where(middle, candidates[0][where, columns], candidates[1][where, columns])


def pair_rows(rank, kept, received, level, layer, layers, before):
    rows, width = kept[0].shape
    count, ways = len(kept), len(received[0])

    def kernel(rank_ref, *refs):
        mine, out = refs[:count], refs[-1]
        totals = (jnp.zeros((8, LANES), jnp.float32),) * 3
        for number, left in enumerate(mine):
            theirs = refs[count + ways * number :][:ways]

            def step(where, columns, totals, left=left, theirs=theirs):
                a = left[where, columns].astype(jnp.float32)
                b = chosen_rows(rank_ref, level, theirs, where, columns).astype(jnp.float32)
                new = [
                    total + (product[:8] + product[8:])
                    for total, product in zip(totals, (a * b, a * a, b * b))
                ]
                return tuple(new)

            totals = tiles(rows, width, step, totals)
        upper = ((rank_ref[0] >> level) & 1) == 1
        dot_value, norm_mine, norm_theirs = [jnp.sum(t, axis=0, keepdims=True) for t in totals]
        out[...] = jnp.zeros_like(out) if before is None else refs[-2][...]
        base = 3 * layer
        out[base : base + 1, :] = dot_value
        out[base + 1 : base + 2, :] = jnp.where(upper, norm_theirs, norm_mine)
        out[base + 2 : base + 3, :] = jnp.where(upper, norm_mine, norm_theirs)

    shape = jax.ShapeDtypeStruct((-(-3 * layers // 8) * 8, LANES), jnp.float32)
    inputs = list(kept) + [part for parts in received for part in parts]
    inputs += [] if before is None else [before]
    return call(kernel, "pair_rows", rank, inputs, [shape])[0]


def pair_combine(rank, sums, kept, received, level):
    layers, count = len(kept), len(kept[0])
    ways = len(received[0][0])
    rows, width = kept[0][0].shape

    def kernel(rank_ref, sums_ref, *refs):
        ins, outs = refs[:-count], refs[-count:]
        totals = jnp.sum(sums_ref[...], axis=1, keepdims=True)
        upper = ((rank_ref[0] >> level) & 1) == 1
        for layer in range(layers):
            dot_value, norm_first, norm_second = [
                totals[3 * layer + k : 3 * layer + k + 1] for k in range(3)
            ]
            first, second = scale_pair(dot_value, norm_first, norm_second)
            mine = jnp.broadcast_to(jnp.where(upper, second, first), (STRIDE, LANES))
            theirs = jnp.broadcast_to(jnp.where(upper, first, second), (STRIDE, LANES))
            for number in range(count):
                left, *others = ins[(1 + ways) * (layer * count + number) :][: 1 + ways]
                out = outs[number]

                def step(where, columns, carry, left=left, others=others, out=out):
                    right = chosen_rows(rank_ref, level, others, where, columns)
                    out[layer, where, columns] = weighted(mine, left[where, columns], theirs, right)
                    return carry

                tiles(rows, width, step, 0)

    shape = jax.ShapeDtypeStruct((layers, rows, width), jnp.bfloat16)
    inputs = [sums]
    for layer in range(layers):
        for left, others in zip(kept[layer], received[layer]):
            inputs += [left] + list(others)
    return call(kernel, "pair_combine", rank, inputs, [shape] * count)


def level_masks(levels):
    masks = [1 << level for level in range(levels)]
    if levels >= 3:
        masks[-1] |= masks[-2]
    return masks


def spread(code, masks):
    value = 0
    for bit, mask in enumerate(masks):
        if code >> bit & 1:
            value ^= mask
    return value


def swap(value, mask, middle=None):
    pairs = [(i, i ^ mask) for i in range(lax.axis_size("rep"))]
    if middle is not None:
        high = mask.bit_length() - 1
        pairs = [(i, j) for i, j in pairs if ((i >> high & 1) != (i >> (high - 1) & 1)) == middle]
    return lax.ppermute(value, "rep", pairs)


def body(activations, output_grads):
    replicas = lax.axis_size("rep")
    par = lax.axis_size("par")
    levels = replicas.bit_length() - 1
    layers, tokens, width = activations.shape
    rows = width // replicas
    rank = lax.axis_index("rep")
    position = jnp.reshape(rank, (1,)).astype(jnp.int32)
    masks = level_masks(levels)
    tails = [tail << 2 for tail in reversed(range(replicas // GROUP))]

    def near_pair(inputs, layer, code):
        return block_pair(position, inputs, output_grads, layer, spread(code, masks), rows)

    own, crossed, far, far_crossed = {}, {}, {}, {}
    rounds = []
    for layer in range(layers):
        codes = [2 | tail for tail in tails] + tails
        second = [(own, far, 2 | tail) for tail in tails]
        second += [(crossed, far_crossed, 2 | tail) for tail in tails]
        rounds += [(layer, code) + unit for code, unit in zip(codes, second)]
    window = 2

    def settle(number, sends):
        layer, code, _, target, block = rounds[number]
        key, other = (layer, code), (layer, block ^ 2)
        sends, (crossed[key], target[other]) = tied(sends, [crossed[key], target[other]])
        return sends

    spans = []
    stride = 1
    while stride < par:
        spans.append(("par", stride))
        stride *= 2

    def summed(value, hops):
        for axis, mask in hops:
            value = value + exchange(value, axis, mask)
        return value

    def layer_gram(layer):
        gram = None
        for tail in tails:
            parts = [held[layer, tail] for held in (own, crossed, far, far_crossed)]
            cost = GRAM_COST if layer == layers - 1 else COST
            gram = gram_rows(position, parts, gram, cost)
        return gram

    def group_result(layer, gram):
        parts = [
            [held[layer, tail] for held in (own, crossed, far, far_crossed)] for tail in tails
        ]
        return dict(zip(tails, group_combine(position, gram, parts)))

    def receive(blocks, level, middle):
        mask = masks[level]
        sends = [blocks[tail | 1 << level] for tail in blocks if not tail >> level & 1]
        if mask == 1 << level:
            return [[swap(sent, mask)] if middle else [] for sent in sends]
        return [[swap(sent, mask, middle)] for sent in sends]

    def receive_all(blocks, level):
        return [a + b for a, b in zip(receive(blocks, level, True), receive(blocks, level, False))]

    def tied_ways(values, ways):
        flat = [part for way in ways for part in way]
        values, flat = tied(values, flat)
        return values, [[flat.pop(0) for _ in way] for way in ways]

    inputs = activations
    per_layer = len(rounds) // layers
    combined, received = [], []
    for number in range(len(rounds)):
        layer, code, source, target, block = rounds[number]
        if number >= 2 * window:
            (inputs,) = settle(number - 2 * window, [inputs])
        own[layer, code], sent = near_pair(inputs, layer, code)
        passed = source[layer, block]
        if number >= window:
            sent, passed = settle(number - window, [sent, passed])
        done, step = divmod(number - window + 1, per_layer)
        if done >= 1 and step == 0:
            gram = layer_gram(done - 1)
            gram = total(
                [gram] + [exchange(gram, "rep", mask) for mask in range(1, GROUP)], CROSS_COST
            )
            combined.append(group_result(done - 1, summed(gram, spans)))
            received.append(receive(combined[-1], 2, True))
        crossed[layer, code] = exchange(sent, "rep", masks[0])
        target[layer, block ^ 2] = exchange(passed, "rep", masks[1])

    first = (layers - 1, tails[0])
    for layer in range(layers - 1):
        names = list(combined[layer])
        values, (own[first],) = tied([combined[layer][tail] for tail in names], [own[first]])
        combined[layer] = dict(zip(names, values))
    gram = summed(layer_gram(layers - 1), [("rep", masks[1])])
    for layer in range(layers - 1):
        names = list(combined[layer])
        values, (gram,) = tied([combined[layer][tail] for tail in names], [gram])
        combined[layer] = dict(zip(names, values))
        outer = receive(combined[layer], 2, False)
        gram = summed(gram, spans[:1])
        (gram,), received[layer] = tied_ways([gram], received[layer])
        received[layer] = [a + b for a, b in zip(received[layer], outer)]
    gram = summed(gram, (spans[1:] if layers > 1 else spans) + [("rep", masks[0])])
    combined.append(group_result(layers - 1, gram))
    names = list(combined[-1])
    values = [combined[-1][tail] for tail in names]
    for layer in range(layers - 1):
        values, received[layer] = tied_ways(values, received[layer])
    combined[-1] = dict(zip(names, values))
    received.append(receive_all(combined[-1], 2))

    for level in range(2, levels):
        keep = [tail for tail in tails if not tail >> level & 1 and tail in combined[0]]
        kept = [[combined[layer][tail] for tail in keep] for layer in range(layers)]
        totals = None
        for layer in range(layers):
            totals = pair_rows(position, kept[layer], received[layer], level, layer, layers, totals)
        totals = summed(totals, spans + [("rep", 1 << bit) for bit in range(level + 1)])
        results = pair_combine(position, totals, kept, received, level)
        if level < levels - 1:
            combined = [
                {tail: result[layer] for tail, result in zip(keep, results)} for layer in range(layers)
            ]
            received = [receive_all(combined[layer], level + 1) for layer in range(layers)]
    return results[0]


def solution(mesh):
    return jax.shard_map(
        body,
        mesh=mesh,
        in_specs=(P(None, "rep", "par"), P(None, "rep", None)),
        out_specs=P(None, ("par", "rep"), None),
        check_vma=False,
    )
```

```python
import jax
import jax.numpy as jnp
from jax import lax
from jax.experimental import pallas as pl
from jax.experimental.pallas import tpu as pltpu
from jax.sharding import PartitionSpec as P

epsilon = 1e-06
LARGE_LIMIT = 60 * 1024 * 1024
SMALL_LIMIT = 16 * 1024 * 1024
LANES = 128
STRIDE = 16
GROUP = 4
GRAM_ROWS = 16
COST = 1024
BLOCK_COST = 1_600_000_000
MESH_HOPS = True
KEPT_COST = 5_000_000_000
BATCHES = ((1, 2), (1,))
FIRST_COST = 3_200_000_000
GRAM_COST = 3_200_000_000
CROSS_COST = 6_000_000_000


def exchange(value, axis, mask):
    return lax.ppermute(value, axis, [(i, i ^ mask) for i in range(lax.axis_size(axis))])


def exchange_all(value, masks):
    if len(masks) == 1:
        ((axis, mask),) = masks.items()
        return exchange(value, axis, mask)
    axes = ("rep", "par")
    inner = lax.axis_size("par")
    pairs = [
        (i * inner + j, (i ^ masks[axes[0]]) * inner + (j ^ masks[axes[1]]))
        for i in range(lax.axis_size(axes[0]))
        for j in range(inner)
    ]
    return lax.ppermute(value, axes, pairs)


def tied(values, others):
    joined = lax.optimization_barrier(tuple(values) + tuple(others))
    return list(joined[: len(values)]), list(joined[len(values) :])


def call(kernel, name, rank, inputs, outputs, flops=COST):
    return pl.pallas_call(
        kernel,
        in_specs=[pl.BlockSpec(memory_space=pltpu.SMEM)]
        + [pl.BlockSpec(memory_space=pltpu.VMEM)] * len(inputs),
        out_specs=[pl.BlockSpec(memory_space=pltpu.VMEM)] * len(outputs),
        out_shape=list(outputs),
        compiler_params=pltpu.CompilerParams(vmem_limit_bytes=SMALL_LIMIT),
        cost_estimate=pl.CostEstimate(flops=flops, bytes_accessed=COST, transcendentals=0),
        name=name,
    )(rank, *inputs)


def block_pairs(rank, activations, output_grads, layer, offsets, rows):
    tokens, width_out = output_grads.shape[1:]
    columns = min(512, width_out)
    count = len(offsets)

    def offset_of(number):
        value = offsets[0]
        for index in range(1, count):
            value = jnp.where(number == index, offsets[index], value)
        return value

    def kernel(rank_ref, a_ref, b_ref, *refs):
        outs, product = refs[:-1], refs[-1]
        number = pl.program_id(1)
        product[...] = lax.dot_general(
            a_ref[0], b_ref[0], (((0,), (0,)), ((), ())), preferred_element_type=jnp.float32
        )
        side = (rank_ref[0] ^ offset_of(number)) & 1
        kept = product[pl.ds(pl.multiple_of(side * rows, rows), rows), :].astype(jnp.bfloat16)
        sent = product[pl.ds(pl.multiple_of((1 - side) * rows, rows), rows), :].astype(jnp.bfloat16)
        for index in range(count):

            @pl.when(number == index)
            def _(index=index):
                outs[2 * index][...] = kept
                outs[2 * index + 1][...] = sent

    shape = jax.ShapeDtypeStruct((rows, width_out), jnp.bfloat16)
    values = pl.pallas_call(
        kernel,
        grid_spec=pltpu.PrefetchScalarGridSpec(
            num_scalar_prefetch=1,
            grid=(width_out // columns, count),
            in_specs=[
                pl.BlockSpec(
                    (1, tokens, 2 * rows), lambda j, i, rank: (layer, 0, (rank[0] ^ offset_of(i)) >> 1)
                ),
                pl.BlockSpec((1, tokens, columns), lambda j, i, rank: (layer, 0, j)),
            ],
            out_specs=[pl.BlockSpec((rows, columns), lambda j, i, rank: (0, j))] * (2 * count),
            scratch_shapes=[pltpu.VMEM((2 * rows, columns), jnp.float32)],
        ),
        out_shape=[shape] * (2 * count),
        compiler_params=pltpu.CompilerParams(vmem_limit_bytes=LARGE_LIMIT),
        cost_estimate=pl.CostEstimate(flops=BLOCK_COST, bytes_accessed=COST, transcendentals=0),
        name="block_pairs",
    )(rank, activations, output_grads)
    return list(zip(values[::2], values[1::2]))


def pair_row(first, second):
    low, high = jnp.minimum(first, second), jnp.maximum(first, second)
    return low * (2 * GROUP - 1 - low) // 2 + high


def tiles(rows, width, step, start):
    def body(index, carry):
        where = pl.ds(pl.multiple_of(index * STRIDE, STRIDE), STRIDE)
        for column in range(0, width, LANES):
            carry = step(where, slice(column, column + LANES), carry)
        return carry

    return lax.fori_loop(0, rows // STRIDE, body, start)


def gram_rows(rank, parts, before, cost):
    rows, width = parts[0].shape
    pairs = [(u, v) for u in range(GROUP) for v in range(u, GROUP)]

    def kernel(rank_ref, *refs):
        ins, out = refs[:GROUP], refs[-1]

        def step(where, columns, totals):
            wide = [ref[where, columns].astype(jnp.float32) for ref in ins]
            new = []
            for total, (u, v) in zip(totals, pairs):
                product = wide[u] * wide[v]
                new.append(total + (product[:8] + product[8:]))
            return tuple(new)

        zero = jnp.zeros((8, LANES), jnp.float32)
        totals = tiles(rows, width, step, (zero,) * len(pairs))
        out[...] = jnp.zeros_like(out) if before is None else refs[GROUP][...]
        mine = rank_ref[0] & (GROUP - 1)
        for total, (u, v) in zip(totals, pairs):
            row = pl.ds(pair_row(mine ^ u, mine ^ v), 1)
            out[row, :] = out[row, :] + jnp.sum(total, axis=0, keepdims=True)

    shape = jax.ShapeDtypeStruct((GRAM_ROWS, LANES), jnp.float32)
    inputs = list(parts) + ([] if before is None else [before])
    return call(kernel, "gram_rows", rank, inputs, [shape], cost)[0]


def total(values, cost):
    def kernel(*refs):
        parts = [ref[...] for ref in refs[:-1]]
        while len(parts) > 1:
            parts = [left + right for left, right in zip(parts[::2], parts[1::2])]
        refs[-1][...] = parts[0]

    return pl.pallas_call(
        kernel,
        in_specs=[pl.BlockSpec(memory_space=pltpu.VMEM)] * len(values),
        out_specs=pl.BlockSpec(memory_space=pltpu.VMEM),
        out_shape=jax.ShapeDtypeStruct(values[0].shape, values[0].dtype),
        compiler_params=pltpu.CompilerParams(vmem_limit_bytes=SMALL_LIMIT),
        cost_estimate=pl.CostEstimate(flops=cost, bytes_accessed=COST, transcendentals=0),
        name="total",
    )(*values)


def scale_pair(dot_value, norm_first, norm_second):
    return (
        1.0 - dot_value / (2.0 * (norm_first + epsilon)),
        1.0 - dot_value / (2.0 * (norm_second + epsilon)),
    )


def weighted(first_scale, first_part, second_scale, second_part):
    result = first_scale * first_part.astype(jnp.float32)
    result = result + second_scale * second_part.astype(jnp.float32)
    return result.astype(jnp.bfloat16)


def group_combine(rank, gram, block_parts, cost=COST):
    rows, width = block_parts[0][0].shape

    def kernel(rank_ref, gram_ref, *refs):
        ins, outs = refs[: GROUP * len(block_parts)], refs[GROUP * len(block_parts) :]
        sums = jnp.sum(gram_ref[...], axis=1, keepdims=True)

        def entry(i, j):
            low, high = min(i, j), max(i, j)
            row = low * (2 * GROUP - 1 - low) // 2 + high
            return sums[row : row + 1]

        def norm(i, j, left, right):
            value = left * left * entry(i, i) + right * right * entry(j, j)
            return jnp.maximum(value + 2.0 * (left * right * entry(i, j)), 0.0)

        low_first, low_second = scale_pair(entry(0, 1), entry(0, 0), entry(1, 1))
        high_first, high_second = scale_pair(entry(2, 3), entry(2, 2), entry(3, 3))
        dot_value = (
            low_first * high_first * entry(0, 2)
            + low_first * high_second * entry(0, 3)
            + low_second * high_first * entry(1, 2)
            + low_second * high_second * entry(1, 3)
        )
        norm_low = norm(0, 1, low_first, low_second)
        norm_high = norm(2, 3, high_first, high_second)
        top_first, top_second = scale_pair(dot_value, norm_low, norm_high)

        odd = (rank_ref[0] & 1) == 1
        upper = (rank_ref[0] & 2) == 2
        low_first, low_second = (
            jnp.where(odd, low_second, low_first),
            jnp.where(odd, low_first, low_second),
        )
        high_first, high_second = (
            jnp.where(odd, high_second, high_first),
            jnp.where(odd, high_first, high_second),
        )
        scales = [
            jnp.where(upper, high_first, low_first),
            jnp.where(upper, high_second, low_second),
            jnp.where(upper, low_first, high_first),
            jnp.where(upper, low_second, high_second),
            jnp.where(upper, top_second, top_first),
            jnp.where(upper, top_first, top_second),
        ]
        scales = [jnp.broadcast_to(scale, (STRIDE, LANES)) for scale in scales]

        for number, out in enumerate(outs):
            block = ins[GROUP * number : GROUP * (number + 1)]

            def step(where, columns, carry, out=out, block=block):
                held = [ref[where, columns] for ref in block]
                near = weighted(scales[0], held[0], scales[1], held[1])
                far = weighted(scales[2], held[2], scales[3], held[3])
                out[where, columns] = weighted(scales[4], near, scales[5], far)
                return carry

            tiles(rows, width, step, 0)

    shape = jax.ShapeDtypeStruct((rows, width), jnp.bfloat16)
    inputs = [gram] + [part for parts in block_parts for part in parts]
    return call(kernel, "group_combine", rank, inputs, [shape] * len(block_parts), cost)


def chosen_rows(rank_ref, level, candidates, where, columns):
    if len(candidates) == 1:
        return candidates[0][where, columns]
    middle = ((rank_ref[0] >> level) & 1) != ((rank_ref[0] >> (level - 1)) & 1)
    return jnp.where(middle, candidates[0][where, columns], candidates[1][where, columns])


def pair_rows(rank, kept, received, level, layer, layers, before):
    rows, width = kept[0].shape
    count, ways = len(kept), len(received[0])

    def kernel(rank_ref, *refs):
        mine, out = refs[:count], refs[-1]
        totals = (jnp.zeros((8, LANES), jnp.float32),) * 3
        for number, left in enumerate(mine):
            theirs = refs[count + ways * number :][:ways]

            def step(where, columns, totals, left=left, theirs=theirs):
                a = left[where, columns].astype(jnp.float32)
                b = chosen_rows(rank_ref, level, theirs, where, columns).astype(jnp.float32)
                new = [
                    total + (product[:8] + product[8:])
                    for total, product in zip(totals, (a * b, a * a, b * b))
                ]
                return tuple(new)

            totals = tiles(rows, width, step, totals)
        upper = ((rank_ref[0] >> level) & 1) == 1
        dot_value, norm_mine, norm_theirs = [jnp.sum(t, axis=0, keepdims=True) for t in totals]
        out[...] = jnp.zeros_like(out) if before is None else refs[-2][...]
        base = 3 * layer
        out[base : base + 1, :] = dot_value
        out[base + 1 : base + 2, :] = jnp.where(upper, norm_theirs, norm_mine)
        out[base + 2 : base + 3, :] = jnp.where(upper, norm_mine, norm_theirs)

    shape = jax.ShapeDtypeStruct((-(-3 * layers // 8) * 8, LANES), jnp.float32)
    inputs = list(kept) + [part for parts in received for part in parts]
    inputs += [] if before is None else [before]
    return call(kernel, "pair_rows", rank, inputs, [shape])[0]


def pair_combine(rank, sums, kept, received, level):
    layers, count = len(kept), len(kept[0])
    ways = len(received[0][0])
    rows, width = kept[0][0].shape

    def kernel(rank_ref, sums_ref, *refs):
        ins, outs = refs[:-count], refs[-count:]
        totals = jnp.sum(sums_ref[...], axis=1, keepdims=True)
        upper = ((rank_ref[0] >> level) & 1) == 1
        for layer in range(layers):
            dot_value, norm_first, norm_second = [
                totals[3 * layer + k : 3 * layer + k + 1] for k in range(3)
            ]
            first, second = scale_pair(dot_value, norm_first, norm_second)
            mine = jnp.broadcast_to(jnp.where(upper, second, first), (STRIDE, LANES))
            theirs = jnp.broadcast_to(jnp.where(upper, first, second), (STRIDE, LANES))
            for number in range(count):
                left, *others = ins[(1 + ways) * (layer * count + number) :][: 1 + ways]
                out = outs[number]

                def step(where, columns, carry, left=left, others=others, out=out):
                    right = chosen_rows(rank_ref, level, others, where, columns)
                    out[layer, where, columns] = weighted(mine, left[where, columns], theirs, right)
                    return carry

                tiles(rows, width, step, 0)

    shape = jax.ShapeDtypeStruct((layers, rows, width), jnp.bfloat16)
    inputs = [sums]
    for layer in range(layers):
        for left, others in zip(kept[layer], received[layer]):
            inputs += [left] + list(others)
    return call(kernel, "pair_combine", rank, inputs, [shape] * count)


def level_masks(levels):
    masks = [1 << level for level in range(levels)]
    if levels >= 3:
        masks[-1] |= masks[-2]
    return masks


def spread(code, masks):
    value = 0
    for bit, mask in enumerate(masks):
        if code >> bit & 1:
            value ^= mask
    return value


def swap(value, mask, middle=None):
    pairs = [(i, i ^ mask) for i in range(lax.axis_size("rep"))]
    if middle is not None:
        high = mask.bit_length() - 1
        pairs = [(i, j) for i, j in pairs if ((i >> high & 1) != (i >> (high - 1) & 1)) == middle]
    return lax.ppermute(value, "rep", pairs)


def body(activations, output_grads):
    replicas = lax.axis_size("rep")
    par = lax.axis_size("par")
    levels = replicas.bit_length() - 1
    layers, tokens, width = activations.shape
    rows = width // replicas
    rank = lax.axis_index("rep")
    position = jnp.reshape(rank, (1,)).astype(jnp.int32)
    masks = level_masks(levels)
    tails = [tail << 2 for tail in reversed(range(replicas // GROUP))]

    own, crossed, far, far_crossed = {}, {}, {}, {}
    rounds = []
    for layer in range(layers):
        codes = [2 | tail for tail in tails] + tails
        second = [(own, far, 2 | tail) for tail in tails]
        second += [(crossed, far_crossed, 2 | tail) for tail in tails]
        rounds += [(layer, code) + unit for code, unit in zip(codes, second)]
    window = 2

    def settle(number, sends):
        layer, code, _, target, block = rounds[number]
        key, other = (layer, code), (layer, block ^ 2)
        sends, (crossed[key], target[other]) = tied(sends, [crossed[key], target[other]])
        return sends

    spans = []
    stride = 1
    while stride < par:
        spans.append([("par", stride)])
        stride *= 2

    def summed(value, hops):
        for hop in hops:
            if len(hop) == 2 and MESH_HOPS:
                first, second = hop
                both = {}
                for axis, mask in hop:
                    both[axis] = both.get(axis, 0) ^ mask
                parts = [value] + [exchange(value, *one) for one in hop] + [exchange_all(value, both)]
                value = total(parts, COST)
            else:
                for axis, mask in hop:
                    value = value + exchange(value, axis, mask)
        return value

    def layer_gram(layer):
        gram = None
        for tail in tails:
            parts = [held[layer, tail] for held in (own, crossed, far, far_crossed)]
            cost = COST if layer < layers - 1 else FIRST_COST if gram is None else GRAM_COST
            gram = gram_rows(position, parts, gram, cost)
        return gram

    def group_result(layer, gram):
        parts = [
            [held[layer, tail] for held in (own, crossed, far, far_crossed)] for tail in tails
        ]
        return {
            tail: group_combine(
                position, gram, [block_parts], KEPT_COST if layer == layers - 1 and tail == 0 else COST
            )[0]
            for tail, block_parts in zip(tails, parts)
        }

    def receive(blocks, level, middle):
        mask = masks[level]
        sends = [blocks[tail | 1 << level] for tail in blocks if not tail >> level & 1]
        if mask == 1 << level:
            return [[swap(sent, mask)] if middle else [] for sent in sends]
        return [[swap(sent, mask, middle)] for sent in sends]

    def receive_all(blocks, level):
        return [a + b for a, b in zip(receive(blocks, level, True), receive(blocks, level, False))]

    def tied_ways(values, ways):
        flat = [part for way in ways for part in way]
        values, flat = tied(values, flat)
        return values, [[flat.pop(0) for _ in way] for way in ways]

    inputs = activations
    per_layer = len(rounds) // layers
    combined, received, sends = [], [], {}

    def multiply(number):
        nonlocal inputs
        if number >= 2 * window:
            (inputs,) = settle(number - 2 * window, [inputs])
        layer = rounds[number][0]
        batch = [number]
        while (batch[-1] + 1) % per_layer and (batch[-1] + 1) % per_layer not in BATCHES[layer > 0]:
            batch.append(batch[-1] + 1)
        offsets = [spread(rounds[index][1], masks) for index in batch]
        values = block_pairs(position, inputs, output_grads, layer, offsets, rows)
        for index, (kept, sent) in zip(batch, values):
            own[layer, rounds[index][1]], sends[index] = kept, sent

    for number in range(len(rounds)):
        layer, code, source, target, block = rounds[number]
        if number not in sends:
            multiply(number)
        sent, passed = sends[number], source[layer, block]
        done, step = divmod(number - window + 1, per_layer)
        if number >= window:
            sent, passed = settle(number - window, [sent, passed])
        if done >= 1 and step == 1:
            (sent, passed), (gram,) = tied([sent, passed], [layer_gram(done - 1)])
            parts = [gram] + [exchange(gram, "rep", mask) for mask in range(1, GROUP)]
            combined.append(group_result(done - 1, summed(total(parts, CROSS_COST), spans)))
            received.append(receive(combined[-1], 2, True))
        crossed[layer, code] = exchange(sent, "rep", masks[0])
        target[layer, block ^ 2] = exchange(passed, "rep", masks[1])

    first = (layers - 1, tails[0])
    for layer in range(layers - 1):
        names = list(combined[layer])
        values = [combined[layer][tail] for tail in names]
        values, (own[first],) = tied(values, [own[first]])
        combined[layer] = dict(zip(names, values))
    gram = summed(layer_gram(layers - 1), [[("rep", masks[1])]])
    for layer in range(layers - 1):
        names = list(combined[layer])
        values, (gram,) = tied([combined[layer][tail] for tail in names], [gram])
        combined[layer] = dict(zip(names, values))
        outer = receive(combined[layer], 2, False)
        gram = summed(gram, spans[:1])
        (gram,), received[layer] = tied_ways([gram], received[layer])
        received[layer] = [a + b for a, b in zip(received[layer], outer)]
    gram = summed(gram, spans[1:-1] + [spans[-1] + [("rep", masks[0])]])
    combined.append(group_result(layers - 1, gram))
    names = [tail for tail in tails if tail >> 2 & 1]
    values = [combined[-1][tail] for tail in names]
    for layer in range(layers - 1):
        values, received[layer] = tied_ways(values, received[layer])
    combined[-1].update(zip(names, values))
    received.append(receive_all(combined[-1], 2))

    for level in range(2, levels):
        keep = [tail for tail in tails if not tail >> level & 1 and tail in combined[0]]
        kept = [[combined[layer][tail] for tail in keep] for layer in range(layers)]
        totals = None
        for layer in range(layers):
            totals = pair_rows(position, kept[layer], received[layer], level, layer, layers, totals)
        bits = [("rep", 1 << bit) for bit in range(level + 1)]
        hops = spans[:-1] + [spans[-1] + bits[:1]] + [bits[i : i + 2] for i in range(1, level + 1, 2)]
        totals = summed(totals, hops)
        results = pair_combine(position, totals, kept, received, level)
        if level < levels - 1:
            combined = [
                {tail: result[layer] for tail, result in zip(keep, results)} for layer in range(layers)
            ]
            received = [receive_all(combined[layer], level + 1) for layer in range(layers)]
    return results[0]


def solution(mesh):
    return jax.shard_map(
        body,
        mesh=mesh,
        in_specs=(P(None, "rep", "par"), P(None, "rep", None)),
        out_specs=P(None, ("par", "rep"), None),
        check_vma=False,
    )
```

```python
import jax
import jax.numpy as jnp
from jax import lax
from jax.experimental import pallas as pl
from jax.experimental.pallas import tpu as pltpu
from jax.sharding import PartitionSpec as P

epsilon = 1e-06
LARGE_LIMIT = 60 * 1024 * 1024
SMALL_LIMIT = 16 * 1024 * 1024
LANES = 128
STRIDE = 16
GROUP = 4
GRAM_ROWS = 16
COST = 1024
BLOCK_COST = 1_600_000_000
MESH_HOPS = True
KEPT_COST = 5_000_000_000
BATCHES = ((1, 2), (1,))
FIRST_COST = 3_200_000_000
GRAM_COST = 3_200_000_000
CROSS_COST = 6_000_000_000


def exchange(value, axis, mask):
    return lax.ppermute(value, axis, [(i, i ^ mask) for i in range(lax.axis_size(axis))])


def exchange_all(value, masks):
    if len(masks) == 1:
        ((axis, mask),) = masks.items()
        return exchange(value, axis, mask)
    axes = ("rep", "par")
    inner = lax.axis_size("par")
    pairs = [
        (i * inner + j, (i ^ masks[axes[0]]) * inner + (j ^ masks[axes[1]]))
        for i in range(lax.axis_size(axes[0]))
        for j in range(inner)
    ]
    return lax.ppermute(value, axes, pairs)


def tied(values, others):
    joined = lax.optimization_barrier(tuple(values) + tuple(others))
    return list(joined[: len(values)]), list(joined[len(values) :])


def call(kernel, name, rank, inputs, outputs, flops=COST):
    return pl.pallas_call(
        kernel,
        in_specs=[pl.BlockSpec(memory_space=pltpu.SMEM)]
        + [pl.BlockSpec(memory_space=pltpu.VMEM)] * len(inputs),
        out_specs=[pl.BlockSpec(memory_space=pltpu.VMEM)] * len(outputs),
        out_shape=list(outputs),
        compiler_params=pltpu.CompilerParams(vmem_limit_bytes=SMALL_LIMIT),
        cost_estimate=pl.CostEstimate(flops=flops, bytes_accessed=COST, transcendentals=0),
        name=name,
    )(rank, *inputs)


def block_pairs(rank, activations, output_grads, layer, offsets, rows):
    tokens, width_out = output_grads.shape[1:]
    columns = min(512, width_out)
    count = len(offsets)

    def offset_of(number):
        value = offsets[0]
        for index in range(1, count):
            value = jnp.where(number == index, offsets[index], value)
        return value

    def kernel(rank_ref, a_ref, b_ref, *refs):
        outs, product = refs[:-1], refs[-1]
        number = pl.program_id(1)
        product[...] = lax.dot_general(
            a_ref[0], b_ref[0], (((0,), (0,)), ((), ())), preferred_element_type=jnp.float32
        )
        side = (rank_ref[0] ^ offset_of(number)) & 1
        kept = product[pl.ds(pl.multiple_of(side * rows, rows), rows), :].astype(jnp.bfloat16)
        sent = product[pl.ds(pl.multiple_of((1 - side) * rows, rows), rows), :].astype(jnp.bfloat16)
        for index in range(count):

            @pl.when(number == index)
            def _(index=index):
                outs[2 * index][...] = kept
                outs[2 * index + 1][...] = sent

    shape = jax.ShapeDtypeStruct((rows, width_out), jnp.bfloat16)
    values = pl.pallas_call(
        kernel,
        grid_spec=pltpu.PrefetchScalarGridSpec(
            num_scalar_prefetch=1,
            grid=(width_out // columns, count),
            in_specs=[
                pl.BlockSpec(
                    (1, tokens, 2 * rows), lambda j, i, rank: (layer, 0, (rank[0] ^ offset_of(i)) >> 1)
                ),
                pl.BlockSpec((1, tokens, columns), lambda j, i, rank: (layer, 0, j)),
            ],
            out_specs=[pl.BlockSpec((rows, columns), lambda j, i, rank: (0, j))] * (2 * count),
            scratch_shapes=[pltpu.VMEM((2 * rows, columns), jnp.float32)],
        ),
        out_shape=[shape] * (2 * count),
        compiler_params=pltpu.CompilerParams(vmem_limit_bytes=LARGE_LIMIT),
        cost_estimate=pl.CostEstimate(flops=BLOCK_COST, bytes_accessed=COST, transcendentals=0),
        name="block_pairs",
    )(rank, activations, output_grads)
    return list(zip(values[::2], values[1::2]))


def tiles(rows, width, step, start):
    def body(index, carry):
        where = pl.ds(pl.multiple_of(index * STRIDE, STRIDE), STRIDE)
        for column in range(0, width, LANES):
            carry = step(where, slice(column, column + LANES), carry)
        return carry

    return lax.fori_loop(0, rows // STRIDE, body, start)


def gram_rows(rank, parts, before, cost):
    rows, width = parts[0].shape

    def kernel(rank_ref, *refs):
        ins, out = refs[:GROUP], refs[-1]

        def step(where, columns, totals):
            wide = [ref[where, columns].astype(jnp.float32) for ref in ins]
            products = []
            for first, second in (wide[:2], wide[2:]):
                both, apart = first + second, first - second
                products += [first * first, second * second, first * second]
                products += [both * both, apart * apart, both * apart]
            products += [first * second for first in wide[:2] for second in wide[2:]]
            return tuple(
                total + (product[:8] + product[8:]) for total, product in zip(totals, products)
            )

        zero = jnp.zeros((8, LANES), jnp.float32)
        totals = tiles(rows, width, step, (zero,) * GRAM_ROWS)
        out[...] = jnp.zeros_like(out) if before is None else refs[GROUP][...]
        odd, upper = rank_ref[0] & 1, (rank_ref[0] >> 1) & 1
        sign = jnp.where(odd == 1, -1.0, 1.0)
        places = []
        for base in (6 * upper, 6 - 6 * upper):
            places += [base + odd, base + 1 - odd] + [base + k for k in range(2, 6)]
        for u in range(2):
            for v in range(2):
                near, far = u ^ odd, v ^ odd
                places.append(12 + jnp.where(upper == 1, 2 * far + near, 2 * near + far))
        for number, (place, value) in enumerate(zip(places, totals)):
            value = jnp.sum(value, axis=0, keepdims=True)
            if number in (5, 11):
                value = sign * value
            out[pl.ds(place, 1), :] = out[pl.ds(place, 1), :] + value

    shape = jax.ShapeDtypeStruct((GRAM_ROWS, LANES), jnp.float32)
    inputs = list(parts) + ([] if before is None else [before])
    return call(kernel, "gram_rows", rank, inputs, [shape], cost)[0]


def total(values, cost):
    def kernel(*refs):
        parts = [ref[...] for ref in refs[:-1]]
        while len(parts) > 1:
            parts = [left + right for left, right in zip(parts[::2], parts[1::2])]
        refs[-1][...] = parts[0]

    return pl.pallas_call(
        kernel,
        in_specs=[pl.BlockSpec(memory_space=pltpu.VMEM)] * len(values),
        out_specs=pl.BlockSpec(memory_space=pltpu.VMEM),
        out_shape=jax.ShapeDtypeStruct(values[0].shape, values[0].dtype),
        compiler_params=pltpu.CompilerParams(vmem_limit_bytes=SMALL_LIMIT),
        cost_estimate=pl.CostEstimate(flops=cost, bytes_accessed=COST, transcendentals=0),
        name="total",
    )(*values)


def scale_pair(dot_value, norm_first, norm_second):
    return (
        1.0 - dot_value / (2.0 * (norm_first + epsilon)),
        1.0 - dot_value / (2.0 * (norm_second + epsilon)),
    )


def weighted(first_scale, first_part, second_scale, second_part):
    result = first_scale * first_part.astype(jnp.float32)
    result = result + second_scale * second_part.astype(jnp.float32)
    return result.astype(jnp.bfloat16)


def group_combine(rank, gram, block_parts, cost=COST):
    rows, width = block_parts[0][0].shape

    def kernel(rank_ref, gram_ref, *refs):
        ins, outs = refs[: GROUP * len(block_parts)], refs[GROUP * len(block_parts) :]
        sums = jnp.sum(gram_ref[...], axis=1, keepdims=True)

        entries = [sums[row : row + 1] for row in range(GRAM_ROWS)]

        def scaled(base):
            first_norm, second_norm, dot_value, both, apart, across = entries[base : base + 6]
            first, second = scale_pair(dot_value, first_norm, second_norm)
            half_sum, half_gap = 0.5 * (first + second), 0.5 * (first - second)
            plain = first * first * first_norm + second * second * second_norm
            plain_cross = 2.0 * (first * second * dot_value)
            turned = half_sum * half_sum * both + half_gap * half_gap * apart
            turned_cross = 2.0 * (half_sum * half_gap * across)
            norm = jnp.where(
                plain + jnp.abs(plain_cross) <= turned + jnp.abs(turned_cross),
                plain + plain_cross,
                turned + turned_cross,
            )
            return first, second, jnp.maximum(norm, 0.0)

        low_first, low_second, norm_low = scaled(0)
        high_first, high_second, norm_high = scaled(6)
        dot_value = low_first * (high_first * entries[12] + high_second * entries[13])
        dot_value = dot_value + low_second * (high_first * entries[14] + high_second * entries[15])
        limit = jnp.sqrt(norm_low) * jnp.sqrt(norm_high)
        dot_value = jnp.clip(dot_value, -limit, limit)
        top_first, top_second = scale_pair(dot_value, norm_low, norm_high)

        odd = (rank_ref[0] & 1) == 1
        upper = (rank_ref[0] & 2) == 2
        low_first, low_second = (
            jnp.where(odd, low_second, low_first),
            jnp.where(odd, low_first, low_second),
        )
        high_first, high_second = (
            jnp.where(odd, high_second, high_first),
            jnp.where(odd, high_first, high_second),
        )
        scales = [
            jnp.where(upper, high_first, low_first),
            jnp.where(upper, high_second, low_second),
            jnp.where(upper, low_first, high_first),
            jnp.where(upper, low_second, high_second),
            jnp.where(upper, top_second, top_first),
            jnp.where(upper, top_first, top_second),
        ]
        scales = [jnp.broadcast_to(scale, (STRIDE, LANES)) for scale in scales]

        for number, out in enumerate(outs):
            block = ins[GROUP * number : GROUP * (number + 1)]

            def step(where, columns, carry, out=out, block=block):
                held = [ref[where, columns] for ref in block]
                near = weighted(scales[0], held[0], scales[1], held[1])
                far = weighted(scales[2], held[2], scales[3], held[3])
                out[where, columns] = weighted(scales[4], near, scales[5], far)
                return carry

            tiles(rows, width, step, 0)

    shape = jax.ShapeDtypeStruct((rows, width), jnp.bfloat16)
    inputs = [gram] + [part for parts in block_parts for part in parts]
    return call(kernel, "group_combine", rank, inputs, [shape] * len(block_parts), cost)


def chosen_rows(rank_ref, level, candidates, where, columns):
    if len(candidates) == 1:
        return candidates[0][where, columns]
    middle = ((rank_ref[0] >> level) & 1) != ((rank_ref[0] >> (level - 1)) & 1)
    return jnp.where(middle, candidates[0][where, columns], candidates[1][where, columns])


def pair_rows(rank, kept, received, level, layer, layers, before):
    rows, width = kept[0].shape
    count, ways = len(kept), len(received[0])

    def kernel(rank_ref, *refs):
        mine, out = refs[:count], refs[-1]
        totals = (jnp.zeros((8, LANES), jnp.float32),) * 3
        for number, left in enumerate(mine):
            theirs = refs[count + ways * number :][:ways]

            def step(where, columns, totals, left=left, theirs=theirs):
                a = left[where, columns].astype(jnp.float32)
                b = chosen_rows(rank_ref, level, theirs, where, columns).astype(jnp.float32)
                new = [
                    total + (product[:8] + product[8:])
                    for total, product in zip(totals, (a * b, a * a, b * b))
                ]
                return tuple(new)

            totals = tiles(rows, width, step, totals)
        upper = ((rank_ref[0] >> level) & 1) == 1
        dot_value, norm_mine, norm_theirs = [jnp.sum(t, axis=0, keepdims=True) for t in totals]
        out[...] = jnp.zeros_like(out) if before is None else refs[-2][...]
        base = 3 * layer
        out[base : base + 1, :] = dot_value
        out[base + 1 : base + 2, :] = jnp.where(upper, norm_theirs, norm_mine)
        out[base + 2 : base + 3, :] = jnp.where(upper, norm_mine, norm_theirs)

    shape = jax.ShapeDtypeStruct((-(-3 * layers // 8) * 8, LANES), jnp.float32)
    inputs = list(kept) + [part for parts in received for part in parts]
    inputs += [] if before is None else [before]
    return call(kernel, "pair_rows", rank, inputs, [shape])[0]


def pair_combine(rank, sums, kept, received, level):
    layers, count = len(kept), len(kept[0])
    ways = len(received[0][0])
    rows, width = kept[0][0].shape

    def kernel(rank_ref, sums_ref, *refs):
        ins, outs = refs[:-count], refs[-count:]
        totals = jnp.sum(sums_ref[...], axis=1, keepdims=True)
        upper = ((rank_ref[0] >> level) & 1) == 1
        for layer in range(layers):
            dot_value, norm_first, norm_second = [
                totals[3 * layer + k : 3 * layer + k + 1] for k in range(3)
            ]
            first, second = scale_pair(dot_value, norm_first, norm_second)
            mine = jnp.broadcast_to(jnp.where(upper, second, first), (STRIDE, LANES))
            theirs = jnp.broadcast_to(jnp.where(upper, first, second), (STRIDE, LANES))
            for number in range(count):
                left, *others = ins[(1 + ways) * (layer * count + number) :][: 1 + ways]
                out = outs[number]

                def step(where, columns, carry, left=left, others=others, out=out):
                    right = chosen_rows(rank_ref, level, others, where, columns)
                    out[layer, where, columns] = weighted(mine, left[where, columns], theirs, right)
                    return carry

                tiles(rows, width, step, 0)

    shape = jax.ShapeDtypeStruct((layers, rows, width), jnp.bfloat16)
    inputs = [sums]
    for layer in range(layers):
        for left, others in zip(kept[layer], received[layer]):
            inputs += [left] + list(others)
    return call(kernel, "pair_combine", rank, inputs, [shape] * count)


def level_masks(levels):
    masks = [1 << level for level in range(levels)]
    if levels >= 3:
        masks[-1] |= masks[-2]
    return masks


def spread(code, masks):
    value = 0
    for bit, mask in enumerate(masks):
        if code >> bit & 1:
            value ^= mask
    return value


def swap(value, mask, middle=None):
    pairs = [(i, i ^ mask) for i in range(lax.axis_size("rep"))]
    if middle is not None:
        high = mask.bit_length() - 1
        pairs = [(i, j) for i, j in pairs if ((i >> high & 1) != (i >> (high - 1) & 1)) == middle]
    return lax.ppermute(value, "rep", pairs)


def body(activations, output_grads):
    replicas = lax.axis_size("rep")
    par = lax.axis_size("par")
    levels = replicas.bit_length() - 1
    layers, tokens, width = activations.shape
    rows = width // replicas
    rank = lax.axis_index("rep")
    position = jnp.reshape(rank, (1,)).astype(jnp.int32)
    masks = level_masks(levels)
    tails = [tail << 2 for tail in reversed(range(replicas // GROUP))]

    own, crossed, far, far_crossed = {}, {}, {}, {}
    rounds = []
    for layer in range(layers):
        codes = [2 | tail for tail in tails] + tails
        second = [(own, far, 2 | tail) for tail in tails]
        second += [(crossed, far_crossed, 2 | tail) for tail in tails]
        rounds += [(layer, code) + unit for code, unit in zip(codes, second)]
    window = 2

    def settle(number, sends):
        layer, code, _, target, block = rounds[number]
        key, other = (layer, code), (layer, block ^ 2)
        sends, (crossed[key], target[other]) = tied(sends, [crossed[key], target[other]])
        return sends

    spans = []
    stride = 1
    while stride < par:
        spans.append([("par", stride)])
        stride *= 2

    def summed(value, hops):
        for hop in hops:
            if len(hop) == 2 and MESH_HOPS:
                first, second = hop
                both = {}
                for axis, mask in hop:
                    both[axis] = both.get(axis, 0) ^ mask
                parts = [value] + [exchange(value, *one) for one in hop] + [exchange_all(value, both)]
                value = total(parts, COST)
            else:
                for axis, mask in hop:
                    value = value + exchange(value, axis, mask)
        return value

    def layer_gram(layer):
        gram = None
        for tail in tails:
            parts = [held[layer, tail] for held in (own, crossed, far, far_crossed)]
            cost = COST if layer < layers - 1 else FIRST_COST if gram is None else GRAM_COST
            gram = gram_rows(position, parts, gram, cost)
        return gram

    def group_result(layer, gram):
        parts = [
            [held[layer, tail] for held in (own, crossed, far, far_crossed)] for tail in tails
        ]
        return {
            tail: group_combine(
                position, gram, [block_parts], KEPT_COST if layer == layers - 1 and tail == 0 else COST
            )[0]
            for tail, block_parts in zip(tails, parts)
        }

    def receive(blocks, level, middle):
        mask = masks[level]
        sends = [blocks[tail | 1 << level] for tail in blocks if not tail >> level & 1]
        if mask == 1 << level:
            return [[swap(sent, mask)] if middle else [] for sent in sends]
        return [[swap(sent, mask, middle)] for sent in sends]

    def receive_all(blocks, level):
        return [a + b for a, b in zip(receive(blocks, level, True), receive(blocks, level, False))]

    def tied_ways(values, ways):
        flat = [part for way in ways for part in way]
        values, flat = tied(values, flat)
        return values, [[flat.pop(0) for _ in way] for way in ways]

    inputs = activations
    per_layer = len(rounds) // layers
    combined, received, sends = [], [], {}

    def multiply(number):
        nonlocal inputs
        if number >= 2 * window:
            (inputs,) = settle(number - 2 * window, [inputs])
        layer = rounds[number][0]
        batch = [number]
        while (batch[-1] + 1) % per_layer and (batch[-1] + 1) % per_layer not in BATCHES[layer > 0]:
            batch.append(batch[-1] + 1)
        offsets = [spread(rounds[index][1], masks) for index in batch]
        values = block_pairs(position, inputs, output_grads, layer, offsets, rows)
        for index, (kept, sent) in zip(batch, values):
            own[layer, rounds[index][1]], sends[index] = kept, sent

    for number in range(len(rounds)):
        layer, code, source, target, block = rounds[number]
        if number not in sends:
            multiply(number)
        sent, passed = sends[number], source[layer, block]
        done, step = divmod(number - window + 1, per_layer)
        if number >= window:
            sent, passed = settle(number - window, [sent, passed])
        if done >= 1 and step == 1:
            (sent, passed), (gram,) = tied([sent, passed], [layer_gram(done - 1)])
            parts = [gram] + [exchange(gram, "rep", mask) for mask in range(1, GROUP)]
            combined.append(group_result(done - 1, summed(total(parts, CROSS_COST), spans)))
            received.append(receive(combined[-1], 2, True))
        crossed[layer, code] = exchange(sent, "rep", masks[0])
        target[layer, block ^ 2] = exchange(passed, "rep", masks[1])

    first = (layers - 1, tails[0])
    for layer in range(layers - 1):
        names = list(combined[layer])
        values = [combined[layer][tail] for tail in names]
        values, (own[first],) = tied(values, [own[first]])
        combined[layer] = dict(zip(names, values))
    gram = summed(layer_gram(layers - 1), [[("rep", masks[1])]])
    for layer in range(layers - 1):
        names = list(combined[layer])
        values, (gram,) = tied([combined[layer][tail] for tail in names], [gram])
        combined[layer] = dict(zip(names, values))
        outer = receive(combined[layer], 2, False)
        gram = summed(gram, spans[:1])
        (gram,), received[layer] = tied_ways([gram], received[layer])
        received[layer] = [a + b for a, b in zip(received[layer], outer)]
    gram = summed(gram, spans[1:-1] + [spans[-1] + [("rep", masks[0])]])
    combined.append(group_result(layers - 1, gram))
    names = [tail for tail in tails if tail >> 2 & 1]
    values = [combined[-1][tail] for tail in names]
    for layer in range(layers - 1):
        values, received[layer] = tied_ways(values, received[layer])
    combined[-1].update(zip(names, values))
    received.append(receive_all(combined[-1], 2))

    for level in range(2, levels):
        keep = [tail for tail in tails if not tail >> level & 1 and tail in combined[0]]
        kept = [[combined[layer][tail] for tail in keep] for layer in range(layers)]
        totals = None
        for layer in range(layers):
            totals = pair_rows(position, kept[layer], received[layer], level, layer, layers, totals)
        bits = [("rep", 1 << bit) for bit in range(level + 1)]
        hops = spans[:-1] + [spans[-1] + bits[:1]] + [bits[i : i + 2] for i in range(1, level + 1, 2)]
        totals = summed(totals, hops)
        results = pair_combine(position, totals, kept, received, level)
        if level < levels - 1:
            combined = [
                {tail: result[layer] for tail, result in zip(keep, results)} for layer in range(layers)
            ]
            received = [receive_all(combined[layer], level + 1) for layer in range(layers)]
    return results[0]


def solution(mesh):
    return jax.shard_map(
        body,
        mesh=mesh,
        in_specs=(P(None, "rep", "par"), P(None, "rep", None)),
        out_specs=P(None, ("par", "rep"), None),
        check_vma=False,
    )
```

```python
import jax
import jax.numpy as jnp
from jax import lax
from jax.experimental import pallas as pl
from jax.experimental.pallas import tpu as pltpu
from jax.sharding import PartitionSpec as P

epsilon = 1e-06
LARGE_LIMIT = 48 * 1024 * 1024
SMALL_LIMIT = 16 * 1024 * 1024
LANES = 128
STRIDE = 16
GROUP = 4
GRAM_ROWS = 16
COST = 1024
BLOCK_COST = 1_600_000_000
MESH_HOPS = True
KEPT_COST = 5_000_000_000
BATCHES = ((1, 2, 3), (1,))
FIRST_COST = 3_200_000_000
GRAM_COST = 3_200_000_000
CROSS_COST = 6_000_000_000


def exchange(value, axis, mask):
    return lax.ppermute(value, axis, [(i, i ^ mask) for i in range(lax.axis_size(axis))])


def exchange_all(value, masks):
    if len(masks) == 1:
        ((axis, mask),) = masks.items()
        return exchange(value, axis, mask)
    axes = ("rep", "par")
    inner = lax.axis_size("par")
    pairs = [
        (i * inner + j, (i ^ masks[axes[0]]) * inner + (j ^ masks[axes[1]]))
        for i in range(lax.axis_size(axes[0]))
        for j in range(inner)
    ]
    return lax.ppermute(value, axes, pairs)


def tied(values, others):
    joined = lax.optimization_barrier(tuple(values) + tuple(others))
    return list(joined[: len(values)]), list(joined[len(values) :])


def call(kernel, name, rank, inputs, outputs, flops=COST):
    return pl.pallas_call(
        kernel,
        in_specs=[pl.BlockSpec(memory_space=pltpu.SMEM)]
        + [pl.BlockSpec(memory_space=pltpu.VMEM)] * len(inputs),
        out_specs=[pl.BlockSpec(memory_space=pltpu.VMEM)] * len(outputs),
        out_shape=list(outputs),
        compiler_params=pltpu.CompilerParams(vmem_limit_bytes=SMALL_LIMIT),
        cost_estimate=pl.CostEstimate(flops=flops, bytes_accessed=COST, transcendentals=0),
        name=name,
    )(rank, *inputs)


def block_pairs(rank, activations, output_grads, layer, offsets, rows):
    tokens, width_out = output_grads.shape[1:]
    columns = min(512, width_out)
    count = len(offsets)

    def offset_of(number):
        value = offsets[0]
        for index in range(1, count):
            value = jnp.where(number == index, offsets[index], value)
        return value

    def kernel(rank_ref, a_ref, b_ref, *refs):
        outs, product = refs[:-1], refs[-1]
        number = pl.program_id(1)
        product[...] = lax.dot_general(
            a_ref[0], b_ref[0], (((0,), (0,)), ((), ())), preferred_element_type=jnp.float32
        )
        side = (rank_ref[0] ^ offset_of(number)) & 1
        kept = product[pl.ds(pl.multiple_of(side * rows, rows), rows), :].astype(jnp.bfloat16)
        sent = product[pl.ds(pl.multiple_of((1 - side) * rows, rows), rows), :].astype(jnp.bfloat16)
        for index in range(count):

            @pl.when(number == index)
            def _(index=index):
                outs[2 * index][...] = kept
                outs[2 * index + 1][...] = sent

    shape = jax.ShapeDtypeStruct((rows, width_out), jnp.bfloat16)
    values = pl.pallas_call(
        kernel,
        grid_spec=pltpu.PrefetchScalarGridSpec(
            num_scalar_prefetch=1,
            grid=(width_out // columns, count),
            in_specs=[
                pl.BlockSpec(
                    (1, tokens, 2 * rows), lambda j, i, rank: (layer, 0, (rank[0] ^ offset_of(i)) >> 1)
                ),
                pl.BlockSpec((1, tokens, columns), lambda j, i, rank: (layer, 0, j)),
            ],
            out_specs=[pl.BlockSpec((rows, columns), lambda j, i, rank: (0, j))] * (2 * count),
            scratch_shapes=[pltpu.VMEM((2 * rows, columns), jnp.float32)],
        ),
        out_shape=[shape] * (2 * count),
        compiler_params=pltpu.CompilerParams(vmem_limit_bytes=LARGE_LIMIT),
        cost_estimate=pl.CostEstimate(flops=BLOCK_COST, bytes_accessed=COST, transcendentals=0),
        name="block_pairs",
    )(rank, activations, output_grads)
    return list(zip(values[::2], values[1::2]))


def tiles(rows, width, step, start):
    def body(index, carry):
        where = pl.ds(pl.multiple_of(index * STRIDE, STRIDE), STRIDE)
        for column in range(0, width, LANES):
            carry = step(where, slice(column, column + LANES), carry)
        return carry

    return lax.fori_loop(0, rows // STRIDE, body, start)


def gram_rows(rank, parts, before, cost):
    rows, width = parts[0].shape

    def kernel(rank_ref, *refs):
        ins, out = refs[:GROUP], refs[-1]

        def step(where, columns, totals):
            wide = [ref[where, columns].astype(jnp.float32) for ref in ins]
            products = []
            for first, second in (wide[:2], wide[2:]):
                both, apart = first + second, first - second
                products += [first * first, second * second, first * second]
                products += [both * both, apart * apart, both * apart]
            products += [first * second for first in wide[:2] for second in wide[2:]]
            return tuple(
                total + (product[:8] + product[8:]) for total, product in zip(totals, products)
            )

        zero = jnp.zeros((8, LANES), jnp.float32)
        totals = tiles(rows, width, step, (zero,) * GRAM_ROWS)
        out[...] = jnp.zeros_like(out) if before is None else refs[GROUP][...]
        odd, upper = rank_ref[0] & 1, (rank_ref[0] >> 1) & 1
        sign = jnp.where(odd == 1, -1.0, 1.0)
        places = []
        for base in (6 * upper, 6 - 6 * upper):
            places += [base + odd, base + 1 - odd] + [base + k for k in range(2, 6)]
        for u in range(2):
            for v in range(2):
                near, far = u ^ odd, v ^ odd
                places.append(12 + jnp.where(upper == 1, 2 * far + near, 2 * near + far))
        for number, (place, value) in enumerate(zip(places, totals)):
            value = jnp.sum(value, axis=0, keepdims=True)
            if number in (5, 11):
                value = sign * value
            out[pl.ds(place, 1), :] = out[pl.ds(place, 1), :] + value

    shape = jax.ShapeDtypeStruct((GRAM_ROWS, LANES), jnp.float32)
    inputs = list(parts) + ([] if before is None else [before])
    return call(kernel, "gram_rows", rank, inputs, [shape], cost)[0]


def total(values, cost):
    def kernel(*refs):
        parts = [ref[...] for ref in refs[:-1]]
        while len(parts) > 1:
            parts = [left + right for left, right in zip(parts[::2], parts[1::2])]
        refs[-1][...] = parts[0]

    return pl.pallas_call(
        kernel,
        in_specs=[pl.BlockSpec(memory_space=pltpu.VMEM)] * len(values),
        out_specs=pl.BlockSpec(memory_space=pltpu.VMEM),
        out_shape=jax.ShapeDtypeStruct(values[0].shape, values[0].dtype),
        compiler_params=pltpu.CompilerParams(vmem_limit_bytes=SMALL_LIMIT),
        cost_estimate=pl.CostEstimate(flops=cost, bytes_accessed=COST, transcendentals=0),
        name="total",
    )(*values)


def scale_pair(dot_value, norm_first, norm_second):
    return (
        1.0 - dot_value / (2.0 * (norm_first + epsilon)),
        1.0 - dot_value / (2.0 * (norm_second + epsilon)),
    )


def weighted(first_scale, first_part, second_scale, second_part):
    result = first_scale * first_part.astype(jnp.float32)
    result = result + second_scale * second_part.astype(jnp.float32)
    return result.astype(jnp.bfloat16)


def group_combine(rank, gram, block_parts, cost=COST):
    rows, width = block_parts[0][0].shape

    def kernel(rank_ref, gram_ref, *refs):
        ins, outs = refs[: GROUP * len(block_parts)], refs[GROUP * len(block_parts) :]
        sums = jnp.sum(gram_ref[...], axis=1, keepdims=True)

        entries = [sums[row : row + 1] for row in range(GRAM_ROWS)]

        def scaled(base):
            first_norm, second_norm, dot_value, both, apart, across = entries[base : base + 6]
            first, second = scale_pair(dot_value, first_norm, second_norm)
            half_sum, half_gap = 0.5 * (first + second), 0.5 * (first - second)
            plain = first * first * first_norm + second * second * second_norm
            plain_cross = 2.0 * (first * second * dot_value)
            turned = half_sum * half_sum * both + half_gap * half_gap * apart
            turned_cross = 2.0 * (half_sum * half_gap * across)
            norm = jnp.where(
                plain + jnp.abs(plain_cross) <= turned + jnp.abs(turned_cross),
                plain + plain_cross,
                turned + turned_cross,
            )
            return first, second, jnp.maximum(norm, 0.0)

        low_first, low_second, norm_low = scaled(0)
        high_first, high_second, norm_high = scaled(6)
        dot_value = low_first * (high_first * entries[12] + high_second * entries[13])
        dot_value = dot_value + low_second * (high_first * entries[14] + high_second * entries[15])
        limit = jnp.sqrt(norm_low) * jnp.sqrt(norm_high)
        dot_value = jnp.clip(dot_value, -limit, limit)
        top_first, top_second = scale_pair(dot_value, norm_low, norm_high)

        odd = (rank_ref[0] & 1) == 1
        upper = (rank_ref[0] & 2) == 2
        low_first, low_second = (
            jnp.where(odd, low_second, low_first),
            jnp.where(odd, low_first, low_second),
        )
        high_first, high_second = (
            jnp.where(odd, high_second, high_first),
            jnp.where(odd, high_first, high_second),
        )
        scales = [
            jnp.where(upper, high_first, low_first),
            jnp.where(upper, high_second, low_second),
            jnp.where(upper, low_first, high_first),
            jnp.where(upper, low_second, high_second),
            jnp.where(upper, top_second, top_first),
            jnp.where(upper, top_first, top_second),
        ]
        scales = [jnp.broadcast_to(scale, (STRIDE, LANES)) for scale in scales]

        for number, out in enumerate(outs):
            block = ins[GROUP * number : GROUP * (number + 1)]

            def step(where, columns, carry, out=out, block=block):
                held = [ref[where, columns] for ref in block]
                near = weighted(scales[0], held[0], scales[1], held[1])
                far = weighted(scales[2], held[2], scales[3], held[3])
                out[where, columns] = weighted(scales[4], near, scales[5], far)
                return carry

            tiles(rows, width, step, 0)

    shape = jax.ShapeDtypeStruct((rows, width), jnp.bfloat16)
    inputs = [gram] + [part for parts in block_parts for part in parts]
    return call(kernel, "group_combine", rank, inputs, [shape] * len(block_parts), cost)


def chosen_rows(rank_ref, level, candidates, where, columns):
    if len(candidates) == 1:
        return candidates[0][where, columns]
    middle = ((rank_ref[0] >> level) & 1) != ((rank_ref[0] >> (level - 1)) & 1)
    return jnp.where(middle, candidates[0][where, columns], candidates[1][where, columns])


def pair_rows(rank, kept, received, level, layer, layers, before):
    rows, width = kept[0].shape
    count, ways = len(kept), len(received[0])

    def kernel(rank_ref, *refs):
        mine, out = refs[:count], refs[-1]
        totals = (jnp.zeros((8, LANES), jnp.float32),) * 3
        for number, left in enumerate(mine):
            theirs = refs[count + ways * number :][:ways]

            def step(where, columns, totals, left=left, theirs=theirs):
                a = left[where, columns].astype(jnp.float32)
                b = chosen_rows(rank_ref, level, theirs, where, columns).astype(jnp.float32)
                new = [
                    total + (product[:8] + product[8:])
                    for total, product in zip(totals, (a * b, a * a, b * b))
                ]
                return tuple(new)

            totals = tiles(rows, width, step, totals)
        upper = ((rank_ref[0] >> level) & 1) == 1
        dot_value, norm_mine, norm_theirs = [jnp.sum(t, axis=0, keepdims=True) for t in totals]
        out[...] = jnp.zeros_like(out) if before is None else refs[-2][...]
        base = 3 * layer
        out[base : base + 1, :] = dot_value
        out[base + 1 : base + 2, :] = jnp.where(upper, norm_theirs, norm_mine)
        out[base + 2 : base + 3, :] = jnp.where(upper, norm_mine, norm_theirs)

    shape = jax.ShapeDtypeStruct((-(-3 * layers // 8) * 8, LANES), jnp.float32)
    inputs = list(kept) + [part for parts in received for part in parts]
    inputs += [] if before is None else [before]
    return call(kernel, "pair_rows", rank, inputs, [shape])[0]


def pair_combine(rank, sums, kept, received, level):
    layers, count = len(kept), len(kept[0])
    ways = len(received[0][0])
    rows, width = kept[0][0].shape

    def kernel(rank_ref, sums_ref, *refs):
        ins, outs = refs[:-count], refs[-count:]
        totals = jnp.sum(sums_ref[...], axis=1, keepdims=True)
        upper = ((rank_ref[0] >> level) & 1) == 1
        for layer in range(layers):
            dot_value, norm_first, norm_second = [
                totals[3 * layer + k : 3 * layer + k + 1] for k in range(3)
            ]
            first, second = scale_pair(dot_value, norm_first, norm_second)
            mine = jnp.broadcast_to(jnp.where(upper, second, first), (STRIDE, LANES))
            theirs = jnp.broadcast_to(jnp.where(upper, first, second), (STRIDE, LANES))
            for number in range(count):
                left, *others = ins[(1 + ways) * (layer * count + number) :][: 1 + ways]
                out = outs[number]

                def step(where, columns, carry, left=left, others=others, out=out):
                    right = chosen_rows(rank_ref, level, others, where, columns)
                    out[layer, where, columns] = weighted(mine, left[where, columns], theirs, right)
                    return carry

                tiles(rows, width, step, 0)

    shape = jax.ShapeDtypeStruct((layers, rows, width), jnp.bfloat16)
    inputs = [sums]
    for layer in range(layers):
        for left, others in zip(kept[layer], received[layer]):
            inputs += [left] + list(others)
    return call(kernel, "pair_combine", rank, inputs, [shape] * count)


def level_masks(levels):
    masks = [1 << level for level in range(levels)]
    if levels >= 3:
        masks[-1] |= masks[-2]
    return masks


def spread(code, masks):
    value = 0
    for bit, mask in enumerate(masks):
        if code >> bit & 1:
            value ^= mask
    return value


def swap(value, mask, middle=None):
    pairs = [(i, i ^ mask) for i in range(lax.axis_size("rep"))]
    if middle is not None:
        high = mask.bit_length() - 1
        pairs = [(i, j) for i, j in pairs if ((i >> high & 1) != (i >> (high - 1) & 1)) == middle]
    return lax.ppermute(value, "rep", pairs)


def body(activations, output_grads):
    replicas = lax.axis_size("rep")
    par = lax.axis_size("par")
    levels = replicas.bit_length() - 1
    layers, tokens, width = activations.shape
    rows = width // replicas
    rank = lax.axis_index("rep")
    position = jnp.reshape(rank, (1,)).astype(jnp.int32)
    masks = level_masks(levels)
    tails = [tail << 2 for tail in reversed(range(replicas // GROUP))]

    own, crossed, far, far_crossed = {}, {}, {}, {}
    rounds = []
    for layer in range(layers):
        codes = [2 | tail for tail in tails] + tails
        second = [(own, far, 2 | tail) for tail in tails]
        second += [(crossed, far_crossed, 2 | tail) for tail in tails]
        rounds += [(layer, code) + unit for code, unit in zip(codes, second)]
    window = 2

    def settle(number, sends):
        layer, code, _, target, block = rounds[number]
        key, other = (layer, code), (layer, block ^ 2)
        sends, (crossed[key], target[other]) = tied(sends, [crossed[key], target[other]])
        return sends

    spans = []
    stride = 1
    while stride < par:
        spans.append([("par", stride)])
        stride *= 2

    def summed(value, hops):
        for hop in hops:
            if len(hop) == 2 and MESH_HOPS:
                first, second = hop
                both = {}
                for axis, mask in hop:
                    both[axis] = both.get(axis, 0) ^ mask
                parts = [value] + [exchange(value, *one) for one in hop] + [exchange_all(value, both)]
                value = total(parts, COST)
            else:
                for axis, mask in hop:
                    value = value + exchange(value, axis, mask)
        return value

    def layer_gram(layer):
        gram = None
        for tail in tails:
            parts = [held[layer, tail] for held in (own, crossed, far, far_crossed)]
            cost = COST if layer < layers - 1 else FIRST_COST if gram is None else GRAM_COST
            gram = gram_rows(position, parts, gram, cost)
        return gram

    def group_result(layer, gram):
        parts = [
            [held[layer, tail] for held in (own, crossed, far, far_crossed)] for tail in tails
        ]
        return {
            tail: group_combine(
                position, gram, [block_parts], KEPT_COST if layer == layers - 1 and tail == 0 else COST
            )[0]
            for tail, block_parts in zip(tails, parts)
        }

    def receive(blocks, level, middle):
        mask = masks[level]
        sends = [blocks[tail | 1 << level] for tail in blocks if not tail >> level & 1]
        if mask == 1 << level:
            return [[swap(sent, mask)] if middle else [] for sent in sends]
        return [[swap(sent, mask, middle)] for sent in sends]

    def receive_all(blocks, level):
        return [a + b for a, b in zip(receive(blocks, level, True), receive(blocks, level, False))]

    def tied_ways(values, ways):
        flat = [part for way in ways for part in way]
        values, flat = tied(values, flat)
        return values, [[flat.pop(0) for _ in way] for way in ways]

    inputs = activations
    per_layer = len(rounds) // layers
    combined, received, sends = [], [], {}

    def multiply(number):
        nonlocal inputs
        if number >= 2 * window:
            (inputs,) = settle(number - 2 * window, [inputs])
        layer = rounds[number][0]
        batch = [number]
        while (batch[-1] + 1) % per_layer and (batch[-1] + 1) % per_layer not in BATCHES[layer > 0]:
            batch.append(batch[-1] + 1)
        offsets = [spread(rounds[index][1], masks) for index in batch]
        values = block_pairs(position, inputs, output_grads, layer, offsets, rows)
        for index, (kept, sent) in zip(batch, values):
            own[layer, rounds[index][1]], sends[index] = kept, sent

    for number in range(len(rounds)):
        layer, code, source, target, block = rounds[number]
        if number not in sends:
            multiply(number)
        sent, passed = sends[number], source[layer, block]
        done, step = divmod(number - window + 1, per_layer)
        if number >= window:
            sent, passed = settle(number - window, [sent, passed])
        if done >= 1 and step == 1:
            (sent, passed), (gram,) = tied([sent, passed], [layer_gram(done - 1)])
            parts = [gram] + [exchange(gram, "rep", mask) for mask in range(1, GROUP)]
            combined.append(group_result(done - 1, summed(total(parts, CROSS_COST), spans)))
            received.append(receive(combined[-1], 2, True))
        crossed[layer, code] = exchange(sent, "rep", masks[0])
        target[layer, block ^ 2] = exchange(passed, "rep", masks[1])

    first = (layers - 1, tails[0])
    for layer in range(layers - 1):
        names = list(combined[layer])
        values = [combined[layer][tail] for tail in names]
        values, (own[first],) = tied(values, [own[first]])
        combined[layer] = dict(zip(names, values))
    gram = summed(layer_gram(layers - 1), [[("rep", masks[1])]])
    for layer in range(layers - 1):
        names = list(combined[layer])
        values, (gram,) = tied([combined[layer][tail] for tail in names], [gram])
        combined[layer] = dict(zip(names, values))
        outer = receive(combined[layer], 2, False)
        gram = summed(gram, spans[:1])
        (gram,), received[layer] = tied_ways([gram], received[layer])
        received[layer] = [a + b for a, b in zip(received[layer], outer)]
    gram = summed(gram, spans[1:-1] + [spans[-1] + [("rep", masks[0])]])
    combined.append(group_result(layers - 1, gram))
    names = [tail for tail in tails if tail >> 2 & 1]
    values = [combined[-1][tail] for tail in names]
    for layer in range(layers - 1):
        values, received[layer] = tied_ways(values, received[layer])
    combined[-1].update(zip(names, values))
    received.append(receive_all(combined[-1], 2))

    for level in range(2, levels):
        keep = [tail for tail in tails if not tail >> level & 1 and tail in combined[0]]
        kept = [[combined[layer][tail] for tail in keep] for layer in range(layers)]
        totals = None
        for layer in range(layers):
            totals = pair_rows(position, kept[layer], received[layer], level, layer, layers, totals)
        bits = [("rep", 1 << bit) for bit in range(level + 1)]
        hops = spans[:-1] + [spans[-1] + bits[:1]] + [bits[i : i + 2] for i in range(1, level + 1, 2)]
        totals = summed(totals, hops)
        results = pair_combine(position, totals, kept, received, level)
        if level < levels - 1:
            combined = [
                {tail: result[layer] for tail, result in zip(keep, results)} for layer in range(layers)
            ]
            received = [receive_all(combined[layer], level + 1) for layer in range(layers)]
    return results[0]


def solution(mesh):
    return jax.shard_map(
        body,
        mesh=mesh,
        in_specs=(P(None, "rep", "par"), P(None, "rep", None)),
        out_specs=P(None, ("par", "rep"), None),
        check_vma=False,
    )
```

```python
import jax
import jax.numpy as jnp
from jax import lax
from jax.experimental import pallas as pl
from jax.experimental.pallas import tpu as pltpu
from jax.sharding import PartitionSpec as P

epsilon = 1e-06
LARGE_LIMIT = 48 * 1024 * 1024
SMALL_LIMIT = 16 * 1024 * 1024
LANES = 128
STRIDE = 16
GROUP = 4
GRAM_ROWS = 16
COST = 1024
BLOCK_COST = 1_600_000_000
MESH_HOPS = True
COPIED = True
CHOSEN = True
KEPT_COST = 5_000_000_000
BATCHES = ((1, 2, 3), (1,))
FIRST_COST = 3_200_000_000
GRAM_COST = 3_200_000_000
CROSS_COST = 6_000_000_000


def exchange(value, axis, mask):
    return lax.ppermute(value, axis, [(i, i ^ mask) for i in range(lax.axis_size(axis))])


def exchange_all(value, masks):
    if len(masks) == 1:
        ((axis, mask),) = masks.items()
        return exchange(value, axis, mask)
    axes = ("rep", "par")
    inner = lax.axis_size("par")
    pairs = [
        (i * inner + j, (i ^ masks[axes[0]]) * inner + (j ^ masks[axes[1]]))
        for i in range(lax.axis_size(axes[0]))
        for j in range(inner)
    ]
    return lax.ppermute(value, axes, pairs)


def tied(values, others):
    joined = lax.optimization_barrier(tuple(values) + tuple(others))
    return list(joined[: len(values)]), list(joined[len(values) :])


def call(kernel, name, rank, inputs, outputs, flops=COST):
    return pl.pallas_call(
        kernel,
        in_specs=[pl.BlockSpec(memory_space=pltpu.SMEM)]
        + [pl.BlockSpec(memory_space=pltpu.VMEM)] * len(inputs),
        out_specs=[pl.BlockSpec(memory_space=pltpu.VMEM)] * len(outputs),
        out_shape=list(outputs),
        compiler_params=pltpu.CompilerParams(vmem_limit_bytes=SMALL_LIMIT),
        cost_estimate=pl.CostEstimate(flops=flops, bytes_accessed=COST, transcendentals=0),
        name=name,
    )(rank, *inputs)


def block_pairs(rank, activations, output_grads, layer, offsets, rows):
    tokens, width_out = output_grads.shape[1:]
    columns = min(512, width_out)
    count = len(offsets)

    def offset_of(number):
        value = offsets[0]
        for index in range(1, count):
            value = jnp.where(number == index, offsets[index], value)
        return value

    def kernel(rank_ref, a_ref, b_ref, *refs):
        outs, product = refs[:-1], refs[-1]
        number = pl.program_id(1)
        product[...] = lax.dot_general(
            a_ref[0], b_ref[0], (((0,), (0,)), ((), ())), preferred_element_type=jnp.float32
        )
        side = (rank_ref[0] ^ offset_of(number)) & 1
        kept = product[pl.ds(pl.multiple_of(side * rows, rows), rows), :].astype(jnp.bfloat16)
        sent = product[pl.ds(pl.multiple_of((1 - side) * rows, rows), rows), :].astype(jnp.bfloat16)
        for index in range(count):

            @pl.when(number == index)
            def _(index=index):
                outs[2 * index][...] = kept
                outs[2 * index + 1][...] = sent

    shape = jax.ShapeDtypeStruct((rows, width_out), jnp.bfloat16)
    values = pl.pallas_call(
        kernel,
        grid_spec=pltpu.PrefetchScalarGridSpec(
            num_scalar_prefetch=1,
            grid=(width_out // columns, count),
            in_specs=[
                pl.BlockSpec(
                    (1, tokens, 2 * rows), lambda j, i, rank: (layer, 0, (rank[0] ^ offset_of(i)) >> 1)
                ),
                pl.BlockSpec((1, tokens, columns), lambda j, i, rank: (layer, 0, j)),
            ],
            out_specs=[pl.BlockSpec((rows, columns), lambda j, i, rank: (0, j))] * (2 * count),
            scratch_shapes=[pltpu.VMEM((2 * rows, columns), jnp.float32)],
        ),
        out_shape=[shape] * (2 * count),
        compiler_params=pltpu.CompilerParams(vmem_limit_bytes=LARGE_LIMIT),
        cost_estimate=pl.CostEstimate(flops=BLOCK_COST, bytes_accessed=COST, transcendentals=0),
        name="block_pairs",
    )(rank, activations, output_grads)
    return list(zip(values[::2], values[1::2]))


def tiles(rows, width, step, start):
    def body(index, carry):
        where = pl.ds(pl.multiple_of(index * STRIDE, STRIDE), STRIDE)
        for column in range(0, width, LANES):
            carry = step(where, slice(column, column + LANES), carry)
        return carry

    return lax.fori_loop(0, rows // STRIDE, body, start)


def gram_rows(rank, parts, before, cost, copied=False):
    rows, width = parts[0].shape

    def kernel(rank_ref, *refs):
        ins, outs = refs[:GROUP], refs[GROUP + (before is not None) :]
        out = outs[0]

        def step(where, columns, totals):
            held = [ref[where, columns] for ref in ins]
            for target, value in zip(outs[1:], held):
                target[where, columns] = value
            wide = [value.astype(jnp.float32) for value in held]
            products = []
            for first, second in (wide[:2], wide[2:]):
                both, apart = first + second, first - second
                products += [first * first, second * second, first * second]
                products += [both * both, apart * apart, both * apart]
            products += [first * second for first in wide[:2] for second in wide[2:]]
            return tuple(
                total + (product[:8] + product[8:]) for total, product in zip(totals, products)
            )

        zero = jnp.zeros((8, LANES), jnp.float32)
        totals = tiles(rows, width, step, (zero,) * GRAM_ROWS)
        out[...] = jnp.zeros_like(out) if before is None else refs[GROUP][...]
        odd, upper = rank_ref[0] & 1, (rank_ref[0] >> 1) & 1
        sign = jnp.where(odd == 1, -1.0, 1.0)
        places = []
        for base in (6 * upper, 6 - 6 * upper):
            places += [base + odd, base + 1 - odd] + [base + k for k in range(2, 6)]
        for u in range(2):
            for v in range(2):
                near, far = u ^ odd, v ^ odd
                places.append(12 + jnp.where(upper == 1, 2 * far + near, 2 * near + far))
        for number, (place, value) in enumerate(zip(places, totals)):
            value = jnp.sum(value, axis=0, keepdims=True)
            if number in (5, 11):
                value = sign * value
            out[pl.ds(place, 1), :] = out[pl.ds(place, 1), :] + value

    shape = jax.ShapeDtypeStruct((GRAM_ROWS, LANES), jnp.float32)
    inputs = list(parts) + ([] if before is None else [before])
    copies = [jax.ShapeDtypeStruct(part.shape, part.dtype) for part in parts] if copied else []
    return call(kernel, "gram_rows", rank, inputs, [shape] + copies, cost)


def total(values, cost):
    def kernel(*refs):
        parts = [ref[...] for ref in refs[:-1]]
        while len(parts) > 1:
            parts = [left + right for left, right in zip(parts[::2], parts[1::2])]
        refs[-1][...] = parts[0]

    return pl.pallas_call(
        kernel,
        in_specs=[pl.BlockSpec(memory_space=pltpu.VMEM)] * len(values),
        out_specs=pl.BlockSpec(memory_space=pltpu.VMEM),
        out_shape=jax.ShapeDtypeStruct(values[0].shape, values[0].dtype),
        compiler_params=pltpu.CompilerParams(vmem_limit_bytes=SMALL_LIMIT),
        cost_estimate=pl.CostEstimate(flops=cost, bytes_accessed=COST, transcendentals=0),
        name="total",
    )(*values)


def scale_pair(dot_value, norm_first, norm_second):
    return (
        1.0 - dot_value / (2.0 * (norm_first + epsilon)),
        1.0 - dot_value / (2.0 * (norm_second + epsilon)),
    )


def weighted(first_scale, first_part, second_scale, second_part):
    result = first_scale * first_part.astype(jnp.float32)
    result = result + second_scale * second_part.astype(jnp.float32)
    return result.astype(jnp.bfloat16)


def group_combine(rank, gram, block_parts, cost=COST):
    rows, width = block_parts[0][0].shape

    def kernel(rank_ref, gram_ref, *refs):
        ins, outs = refs[: GROUP * len(block_parts)], refs[GROUP * len(block_parts) :]
        sums = jnp.sum(gram_ref[...], axis=1, keepdims=True)

        entries = [sums[row : row + 1] for row in range(GRAM_ROWS)]

        def scaled(base):
            first_norm, second_norm, dot_value, both, apart, across = entries[base : base + 6]
            first, second = scale_pair(dot_value, first_norm, second_norm)
            half_sum, half_gap = 0.5 * (first + second), 0.5 * (first - second)
            plain = first * first * first_norm + second * second * second_norm
            plain_cross = 2.0 * (first * second * dot_value)
            turned = half_sum * half_sum * both + half_gap * half_gap * apart
            turned_cross = 2.0 * (half_sum * half_gap * across)
            norm = jnp.where(
                plain + jnp.abs(plain_cross) <= turned + jnp.abs(turned_cross),
                plain + plain_cross,
                turned + turned_cross,
            )
            return first, second, jnp.maximum(norm, 0.0)

        low_first, low_second, norm_low = scaled(0)
        high_first, high_second, norm_high = scaled(6)
        dot_value = low_first * (high_first * entries[12] + high_second * entries[13])
        dot_value = dot_value + low_second * (high_first * entries[14] + high_second * entries[15])
        limit = jnp.sqrt(norm_low) * jnp.sqrt(norm_high)
        dot_value = jnp.clip(dot_value, -limit, limit)
        top_first, top_second = scale_pair(dot_value, norm_low, norm_high)

        odd = (rank_ref[0] & 1) == 1
        upper = (rank_ref[0] & 2) == 2
        low_first, low_second = (
            jnp.where(odd, low_second, low_first),
            jnp.where(odd, low_first, low_second),
        )
        high_first, high_second = (
            jnp.where(odd, high_second, high_first),
            jnp.where(odd, high_first, high_second),
        )
        scales = [
            jnp.where(upper, high_first, low_first),
            jnp.where(upper, high_second, low_second),
            jnp.where(upper, low_first, high_first),
            jnp.where(upper, low_second, high_second),
            jnp.where(upper, top_second, top_first),
            jnp.where(upper, top_first, top_second),
        ]
        scales = [jnp.broadcast_to(scale, (STRIDE, LANES)) for scale in scales]

        for number, out in enumerate(outs):
            block = ins[GROUP * number : GROUP * (number + 1)]

            def step(where, columns, carry, out=out, block=block):
                held = [ref[where, columns] for ref in block]
                near = weighted(scales[0], held[0], scales[1], held[1])
                far = weighted(scales[2], held[2], scales[3], held[3])
                out[where, columns] = weighted(scales[4], near, scales[5], far)
                return carry

            tiles(rows, width, step, 0)

    shape = jax.ShapeDtypeStruct((rows, width), jnp.bfloat16)
    inputs = [gram] + [part for parts in block_parts for part in parts]
    return call(kernel, "group_combine", rank, inputs, [shape] * len(block_parts), cost)


def chosen_rows(rank_ref, level, candidates, where, columns):
    if len(candidates) == 1:
        return candidates[0][where, columns]
    middle = ((rank_ref[0] >> level) & 1) != ((rank_ref[0] >> (level - 1)) & 1)
    return jnp.where(middle, candidates[0][where, columns], candidates[1][where, columns])


def pair_rows(rank, kept, received, level, layer, layers, before):
    rows, width = kept[0].shape
    count, ways = len(kept), len(received[0])
    chooses = CHOSEN and ways > 1

    def kernel(rank_ref, *refs):
        mine = refs[:count]
        inputs_end = count + count * ways + (before is not None)
        out, chosen = refs[inputs_end], refs[inputs_end + 1 :]
        totals = (jnp.zeros((8, LANES), jnp.float32),) * 3
        for number, left in enumerate(mine):
            theirs = refs[count + ways * number :][:ways]

            def step(where, columns, totals, left=left, theirs=theirs, number=number):
                a = left[where, columns].astype(jnp.float32)
                b = chosen_rows(rank_ref, level, theirs, where, columns)
                if chooses:
                    chosen[number][where, columns] = b
                b = b.astype(jnp.float32)
                new = [
                    total + (product[:8] + product[8:])
                    for total, product in zip(totals, (a * b, a * a, b * b))
                ]
                return tuple(new)

            totals = tiles(rows, width, step, totals)
        upper = ((rank_ref[0] >> level) & 1) == 1
        dot_value, norm_mine, norm_theirs = [jnp.sum(t, axis=0, keepdims=True) for t in totals]
        out[...] = jnp.zeros_like(out) if before is None else refs[inputs_end - 1][...]
        base = 3 * layer
        out[base : base + 1, :] = dot_value
        out[base + 1 : base + 2, :] = jnp.where(upper, norm_theirs, norm_mine)
        out[base + 2 : base + 3, :] = jnp.where(upper, norm_mine, norm_theirs)

    shapes = [jax.ShapeDtypeStruct((-(-3 * layers // 8) * 8, LANES), jnp.float32)]
    if chooses:
        shapes += [jax.ShapeDtypeStruct((rows, width), jnp.bfloat16)] * count
    inputs = list(kept) + [part for parts in received for part in parts]
    inputs += [] if before is None else [before]
    sums, *chosen = call(kernel, "pair_rows", rank, inputs, shapes)
    return sums, [[part] for part in chosen] if chooses else received


def pair_combine(rank, sums, kept, received, level):
    layers, count = len(kept), len(kept[0])
    ways = len(received[0][0])
    rows, width = kept[0][0].shape

    def kernel(rank_ref, sums_ref, *refs):
        ins, outs = refs[:-count], refs[-count:]
        totals = jnp.sum(sums_ref[...], axis=1, keepdims=True)
        upper = ((rank_ref[0] >> level) & 1) == 1
        for layer in range(layers):
            dot_value, norm_first, norm_second = [
                totals[3 * layer + k : 3 * layer + k + 1] for k in range(3)
            ]
            first, second = scale_pair(dot_value, norm_first, norm_second)
            mine = jnp.broadcast_to(jnp.where(upper, second, first), (STRIDE, LANES))
            theirs = jnp.broadcast_to(jnp.where(upper, first, second), (STRIDE, LANES))
            for number in range(count):
                left, *others = ins[(1 + ways) * (layer * count + number) :][: 1 + ways]
                out = outs[number]

                def step(where, columns, carry, left=left, others=others, out=out):
                    right = chosen_rows(rank_ref, level, others, where, columns)
                    out[layer, where, columns] = weighted(mine, left[where, columns], theirs, right)
                    return carry

                tiles(rows, width, step, 0)

    shape = jax.ShapeDtypeStruct((layers, rows, width), jnp.bfloat16)
    inputs = [sums]
    for layer in range(layers):
        for left, others in zip(kept[layer], received[layer]):
            inputs += [left] + list(others)
    return call(kernel, "pair_combine", rank, inputs, [shape] * count)


def level_masks(levels):
    masks = [1 << level for level in range(levels)]
    if levels >= 3:
        masks[-1] |= masks[-2]
    return masks


def spread(code, masks):
    value = 0
    for bit, mask in enumerate(masks):
        if code >> bit & 1:
            value ^= mask
    return value


def swap(value, mask, middle=None):
    pairs = [(i, i ^ mask) for i in range(lax.axis_size("rep"))]
    if middle is not None:
        high = mask.bit_length() - 1
        pairs = [(i, j) for i, j in pairs if ((i >> high & 1) != (i >> (high - 1) & 1)) == middle]
    return lax.ppermute(value, "rep", pairs)


def body(activations, output_grads):
    replicas = lax.axis_size("rep")
    par = lax.axis_size("par")
    levels = replicas.bit_length() - 1
    layers, tokens, width = activations.shape
    rows = width // replicas
    rank = lax.axis_index("rep")
    position = jnp.reshape(rank, (1,)).astype(jnp.int32)
    masks = level_masks(levels)
    tails = [tail << 2 for tail in reversed(range(replicas // GROUP))]

    own, crossed, far, far_crossed = {}, {}, {}, {}
    rounds = []
    for layer in range(layers):
        codes = [2 | tail for tail in tails] + tails
        second = [(own, far, 2 | tail) for tail in tails]
        second += [(crossed, far_crossed, 2 | tail) for tail in tails]
        rounds += [(layer, code) + unit for code, unit in zip(codes, second)]
    window = 2

    def settle(number, sends):
        layer, code, _, target, block = rounds[number]
        key, other = (layer, code), (layer, block ^ 2)
        sends, (crossed[key], target[other]) = tied(sends, [crossed[key], target[other]])
        return sends

    spans = []
    stride = 1
    while stride < par:
        spans.append([("par", stride)])
        stride *= 2

    def summed(value, hops):
        for hop in hops:
            if len(hop) == 2 and MESH_HOPS:
                first, second = hop
                both = {}
                for axis, mask in hop:
                    both[axis] = both.get(axis, 0) ^ mask
                parts = [value] + [exchange(value, *one) for one in hop] + [exchange_all(value, both)]
                value = total(parts, COST)
            else:
                for axis, mask in hop:
                    value = value + exchange(value, axis, mask)
        return value

    def layer_gram(layer):
        gram = None
        for tail in tails:
            parts = [held[layer, tail] for held in (own, crossed, far, far_crossed)]
            cost = COST if layer < layers - 1 else FIRST_COST if gram is None else GRAM_COST
            copied = COPIED and layer == layers - 1 and gram is None
            gram, *copies = gram_rows(position, parts, gram, cost, copied)
            for held, copy in zip((own, crossed, far, far_crossed), copies):
                held[layer, tail] = copy
        return gram

    def group_result(layer, gram):
        parts = [
            [held[layer, tail] for held in (own, crossed, far, far_crossed)] for tail in tails
        ]
        return {
            tail: group_combine(
                position, gram, [block_parts], KEPT_COST if layer == layers - 1 and tail == 0 else COST
            )[0]
            for tail, block_parts in zip(tails, parts)
        }

    def receive(blocks, level, middle):
        mask = masks[level]
        sends = [blocks[tail | 1 << level] for tail in blocks if not tail >> level & 1]
        if mask == 1 << level:
            return [[swap(sent, mask)] if middle else [] for sent in sends]
        return [[swap(sent, mask, middle)] for sent in sends]

    def receive_all(blocks, level):
        return [a + b for a, b in zip(receive(blocks, level, True), receive(blocks, level, False))]

    def tied_ways(values, ways):
        flat = [part for way in ways for part in way]
        values, flat = tied(values, flat)
        return values, [[flat.pop(0) for _ in way] for way in ways]

    inputs = activations
    per_layer = len(rounds) // layers
    combined, received, sends = [], [], {}

    def multiply(number):
        nonlocal inputs
        if number >= 2 * window:
            (inputs,) = settle(number - 2 * window, [inputs])
        layer = rounds[number][0]
        batch = [number]
        while (batch[-1] + 1) % per_layer and (batch[-1] + 1) % per_layer not in BATCHES[layer > 0]:
            batch.append(batch[-1] + 1)
        offsets = [spread(rounds[index][1], masks) for index in batch]
        values = block_pairs(position, inputs, output_grads, layer, offsets, rows)
        for index, (kept, sent) in zip(batch, values):
            own[layer, rounds[index][1]], sends[index] = kept, sent

    for number in range(len(rounds)):
        layer, code, source, target, block = rounds[number]
        if number not in sends:
            multiply(number)
        sent, passed = sends[number], source[layer, block]
        done, step = divmod(number - window + 1, per_layer)
        if number >= window:
            sent, passed = settle(number - window, [sent, passed])
        if done >= 1 and step == 1:
            (sent, passed), (gram,) = tied([sent, passed], [layer_gram(done - 1)])
            parts = [gram] + [exchange(gram, "rep", mask) for mask in range(1, GROUP)]
            combined.append(group_result(done - 1, summed(total(parts, CROSS_COST), spans)))
            received.append(receive(combined[-1], 2, True))
        crossed[layer, code] = exchange(sent, "rep", masks[0])
        target[layer, block ^ 2] = exchange(passed, "rep", masks[1])

    first = (layers - 1, tails[0])
    for layer in range(layers - 1):
        names = list(combined[layer])
        values = [combined[layer][tail] for tail in names]
        values, (own[first],) = tied(values, [own[first]])
        combined[layer] = dict(zip(names, values))
    gram = summed(layer_gram(layers - 1), [[("rep", masks[1])]])
    for layer in range(layers - 1):
        names = list(combined[layer])
        values, (gram,) = tied([combined[layer][tail] for tail in names], [gram])
        combined[layer] = dict(zip(names, values))
        outer = receive(combined[layer], 2, False)
        gram = summed(gram, spans[:1])
        (gram,), received[layer] = tied_ways([gram], received[layer])
        received[layer] = [a + b for a, b in zip(received[layer], outer)]
    gram = summed(gram, spans[1:-1] + [spans[-1] + [("rep", masks[0])]])
    combined.append(group_result(layers - 1, gram))
    names = [tail for tail in tails if tail >> 2 & 1]
    values = [combined[-1][tail] for tail in names]
    for layer in range(layers - 1):
        values, received[layer] = tied_ways(values, received[layer])
    combined[-1].update(zip(names, values))
    received.append(receive_all(combined[-1], 2))

    for level in range(2, levels):
        keep = [tail for tail in tails if not tail >> level & 1 and tail in combined[0]]
        kept = [[combined[layer][tail] for tail in keep] for layer in range(layers)]
        totals = None
        for layer in range(layers):
            totals, received[layer] = pair_rows(
                position, kept[layer], received[layer], level, layer, layers, totals
            )
        bits = [("rep", 1 << bit) for bit in range(level + 1)]
        hops = spans[:-1] + [spans[-1] + bits[:1]] + [bits[i : i + 2] for i in range(1, level + 1, 2)]
        totals = summed(totals, hops)
        results = pair_combine(position, totals, kept, received, level)
        if level < levels - 1:
            combined = [
                {tail: result[layer] for tail, result in zip(keep, results)} for layer in range(layers)
            ]
            received = [receive_all(combined[layer], level + 1) for layer in range(layers)]
    return results[0]


def solution(mesh):
    return jax.shard_map(
        body,
        mesh=mesh,
        in_specs=(P(None, "rep", "par"), P(None, "rep", None)),
        out_specs=P(None, ("par", "rep"), None),
        check_vma=False,
    )
```

```python
import jax
import jax.numpy as jnp
from jax import lax
from jax.experimental import pallas as pl
from jax.experimental.pallas import tpu as pltpu
from jax.sharding import PartitionSpec as P

epsilon = 1e-06
LARGE_LIMIT = 48 * 1024 * 1024
SMALL_LIMIT = 16 * 1024 * 1024
LANES = 128
STRIDE = 16
GROUP = 4
GRAM_ROWS = 16
COST = 1024
BLOCK_COST = 1_600_000_000
MESH_HOPS = True
KEPT_COST = 5_000_000_000
BATCHES = ((1, 2, 3), (1,))
FIRST_COST = 3_200_000_000
GRAM_COST = 3_200_000_000
CROSS_COST = 6_000_000_000


def exchange(value, axis, mask):
    return lax.ppermute(value, axis, [(i, i ^ mask) for i in range(lax.axis_size(axis))])


def exchange_all(value, masks):
    if len(masks) == 1:
        ((axis, mask),) = masks.items()
        return exchange(value, axis, mask)
    axes = ("rep", "par")
    inner = lax.axis_size("par")
    pairs = [
        (i * inner + j, (i ^ masks[axes[0]]) * inner + (j ^ masks[axes[1]]))
        for i in range(lax.axis_size(axes[0]))
        for j in range(inner)
    ]
    return lax.ppermute(value, axes, pairs)


def tied(values, others):
    joined = lax.optimization_barrier(tuple(values) + tuple(others))
    return list(joined[: len(values)]), list(joined[len(values) :])


def call(kernel, name, rank, inputs, outputs, flops=COST):
    return pl.pallas_call(
        kernel,
        in_specs=[pl.BlockSpec(memory_space=pltpu.SMEM)]
        + [pl.BlockSpec(memory_space=pltpu.VMEM)] * len(inputs),
        out_specs=[pl.BlockSpec(memory_space=pltpu.VMEM)] * len(outputs),
        out_shape=list(outputs),
        compiler_params=pltpu.CompilerParams(vmem_limit_bytes=SMALL_LIMIT),
        cost_estimate=pl.CostEstimate(flops=flops, bytes_accessed=COST, transcendentals=0),
        name=name,
    )(rank, *inputs)


def block_pairs(rank, activations, output_grads, layer, offsets, rows):
    tokens, width_out = output_grads.shape[1:]
    columns = min(512, width_out)
    count = len(offsets)

    def offset_of(number):
        value = offsets[0]
        for index in range(1, count):
            value = jnp.where(number == index, offsets[index], value)
        return value

    def kernel(rank_ref, a_ref, b_ref, *refs):
        outs, product = refs[:-1], refs[-1]
        number = pl.program_id(1)
        product[...] = lax.dot_general(
            a_ref[0], b_ref[0], (((0,), (0,)), ((), ())), preferred_element_type=jnp.float32
        )
        side = (rank_ref[0] ^ offset_of(number)) & 1
        kept = product[pl.ds(pl.multiple_of(side * rows, rows), rows), :].astype(jnp.bfloat16)
        sent = product[pl.ds(pl.multiple_of((1 - side) * rows, rows), rows), :].astype(jnp.bfloat16)
        for index in range(count):

            @pl.when(number == index)
            def _(index=index):
                outs[2 * index][...] = kept
                outs[2 * index + 1][...] = sent

    shape = jax.ShapeDtypeStruct((rows, width_out), jnp.bfloat16)
    values = pl.pallas_call(
        kernel,
        grid_spec=pltpu.PrefetchScalarGridSpec(
            num_scalar_prefetch=1,
            grid=(width_out // columns, count),
            in_specs=[
                pl.BlockSpec(
                    (1, tokens, 2 * rows), lambda j, i, rank: (layer, 0, (rank[0] ^ offset_of(i)) >> 1)
                ),
                pl.BlockSpec((1, tokens, columns), lambda j, i, rank: (layer, 0, j)),
            ],
            out_specs=[pl.BlockSpec((rows, columns), lambda j, i, rank: (0, j))] * (2 * count),
            scratch_shapes=[pltpu.VMEM((2 * rows, columns), jnp.float32)],
        ),
        out_shape=[shape] * (2 * count),
        compiler_params=pltpu.CompilerParams(vmem_limit_bytes=LARGE_LIMIT),
        cost_estimate=pl.CostEstimate(flops=BLOCK_COST, bytes_accessed=COST, transcendentals=0),
        name="block_pairs",
    )(rank, activations, output_grads)
    return list(zip(values[::2], values[1::2]))


def tiles(rows, width, step, start):
    def body(index, carry):
        where = pl.ds(pl.multiple_of(index * STRIDE, STRIDE), STRIDE)
        for column in range(0, width, LANES):
            carry = step(where, slice(column, column + LANES), carry)
        return carry

    return lax.fori_loop(0, rows // STRIDE, body, start)


def gram_rows(rank, parts, before, cost):
    rows, width = parts[0].shape

    def kernel(rank_ref, *refs):
        ins, out = refs[:GROUP], refs[-1]

        def step(where, columns, totals):
            wide = [ref[where, columns].astype(jnp.float32) for ref in ins]
            products = []
            for first, second in (wide[:2], wide[2:]):
                both, apart = first + second, first - second
                products += [first * first, second * second, first * second]
                products += [both * both, apart * apart, both * apart]
            products += [first * second for first in wide[:2] for second in wide[2:]]
            return tuple(
                total + (product[:8] + product[8:]) for total, product in zip(totals, products)
            )

        zero = jnp.zeros((8, LANES), jnp.float32)
        totals = tiles(rows, width, step, (zero,) * GRAM_ROWS)
        out[...] = jnp.zeros_like(out) if before is None else refs[GROUP][...]
        odd, upper = rank_ref[0] & 1, (rank_ref[0] >> 1) & 1
        sign = jnp.where(odd == 1, -1.0, 1.0)
        places = []
        for base in (6 * upper, 6 - 6 * upper):
            places += [base + odd, base + 1 - odd] + [base + k for k in range(2, 6)]
        for u in range(2):
            for v in range(2):
                near, far = u ^ odd, v ^ odd
                places.append(12 + jnp.where(upper == 1, 2 * far + near, 2 * near + far))
        for number, (place, value) in enumerate(zip(places, totals)):
            value = jnp.sum(value, axis=0, keepdims=True)
            if number in (5, 11):
                value = sign * value
            out[pl.ds(place, 1), :] = out[pl.ds(place, 1), :] + value

    shape = jax.ShapeDtypeStruct((GRAM_ROWS, LANES), jnp.float32)
    inputs = list(parts) + ([] if before is None else [before])
    return call(kernel, "gram_rows", rank, inputs, [shape], cost)[0]


def total(values, cost):
    def kernel(*refs):
        parts = [ref[...] for ref in refs[:-1]]
        while len(parts) > 1:
            parts = [left + right for left, right in zip(parts[::2], parts[1::2])]
        refs[-1][...] = parts[0]

    return pl.pallas_call(
        kernel,
        in_specs=[pl.BlockSpec(memory_space=pltpu.VMEM)] * len(values),
        out_specs=pl.BlockSpec(memory_space=pltpu.VMEM),
        out_shape=jax.ShapeDtypeStruct(values[0].shape, values[0].dtype),
        compiler_params=pltpu.CompilerParams(vmem_limit_bytes=SMALL_LIMIT),
        cost_estimate=pl.CostEstimate(flops=cost, bytes_accessed=COST, transcendentals=0),
        name="total",
    )(*values)


def scale_pair(dot_value, norm_first, norm_second):
    return (
        1.0 - dot_value / (2.0 * (norm_first + epsilon)),
        1.0 - dot_value / (2.0 * (norm_second + epsilon)),
    )


def weighted(first_scale, first_part, second_scale, second_part):
    result = first_scale * first_part.astype(jnp.float32)
    result = result + second_scale * second_part.astype(jnp.float32)
    return result.astype(jnp.bfloat16)


def group_combine(rank, gram, block_parts, cost=COST):
    rows, width = block_parts[0][0].shape

    def kernel(rank_ref, gram_ref, *refs):
        ins, outs = refs[: GROUP * len(block_parts)], refs[GROUP * len(block_parts) :]
        sums = jnp.sum(gram_ref[...], axis=1, keepdims=True)

        entries = [sums[row : row + 1] for row in range(GRAM_ROWS)]

        def scaled(base):
            first_norm, second_norm, dot_value, both, apart, across = entries[base : base + 6]
            first, second = scale_pair(dot_value, first_norm, second_norm)
            half_sum, half_gap = 0.5 * (first + second), 0.5 * (first - second)
            plain = first * first * first_norm + second * second * second_norm
            plain_cross = 2.0 * (first * second * dot_value)
            turned = half_sum * half_sum * both + half_gap * half_gap * apart
            turned_cross = 2.0 * (half_sum * half_gap * across)
            norm = jnp.where(
                plain + jnp.abs(plain_cross) <= turned + jnp.abs(turned_cross),
                plain + plain_cross,
                turned + turned_cross,
            )
            return first, second, jnp.maximum(norm, 0.0)

        low_first, low_second, norm_low = scaled(0)
        high_first, high_second, norm_high = scaled(6)
        dot_value = low_first * (high_first * entries[12] + high_second * entries[13])
        dot_value = dot_value + low_second * (high_first * entries[14] + high_second * entries[15])
        limit = jnp.sqrt(norm_low) * jnp.sqrt(norm_high)
        dot_value = jnp.clip(dot_value, -limit, limit)
        top_first, top_second = scale_pair(dot_value, norm_low, norm_high)

        odd = (rank_ref[0] & 1) == 1
        upper = (rank_ref[0] & 2) == 2
        low_first, low_second = (
            jnp.where(odd, low_second, low_first),
            jnp.where(odd, low_first, low_second),
        )
        high_first, high_second = (
            jnp.where(odd, high_second, high_first),
            jnp.where(odd, high_first, high_second),
        )
        scales = [
            jnp.where(upper, high_first, low_first),
            jnp.where(upper, high_second, low_second),
            jnp.where(upper, low_first, high_first),
            jnp.where(upper, low_second, high_second),
            jnp.where(upper, top_second, top_first),
            jnp.where(upper, top_first, top_second),
        ]
        scales = [jnp.broadcast_to(scale, (STRIDE, LANES)) for scale in scales]

        for number, out in enumerate(outs):
            block = ins[GROUP * number : GROUP * (number + 1)]

            def step(where, columns, carry, out=out, block=block):
                held = [ref[where, columns] for ref in block]
                near = weighted(scales[0], held[0], scales[1], held[1])
                far = weighted(scales[2], held[2], scales[3], held[3])
                out[where, columns] = weighted(scales[4], near, scales[5], far)
                return carry

            tiles(rows, width, step, 0)

    shape = jax.ShapeDtypeStruct((rows, width), jnp.bfloat16)
    inputs = [gram] + [part for parts in block_parts for part in parts]
    return call(kernel, "group_combine", rank, inputs, [shape] * len(block_parts), cost)


def chosen_rows(rank_ref, level, candidates, where, columns):
    if len(candidates) == 1:
        return candidates[0][where, columns]
    middle = ((rank_ref[0] >> level) & 1) != ((rank_ref[0] >> (level - 1)) & 1)
    return jnp.where(middle, candidates[0][where, columns], candidates[1][where, columns])


def pair_rows(rank, kept, received, level, layer, layers, before):
    rows, width = kept[0].shape
    count, ways = len(kept), len(received[0])

    def kernel(rank_ref, *refs):
        mine, out = refs[:count], refs[-1]
        totals = (jnp.zeros((8, LANES), jnp.float32),) * 3
        for number, left in enumerate(mine):
            theirs = refs[count + ways * number :][:ways]

            def step(where, columns, totals, left=left, theirs=theirs):
                a = left[where, columns].astype(jnp.float32)
                b = chosen_rows(rank_ref, level, theirs, where, columns).astype(jnp.float32)
                new = [
                    total + (product[:8] + product[8:])
                    for total, product in zip(totals, (a * b, a * a, b * b))
                ]
                return tuple(new)

            totals = tiles(rows, width, step, totals)
        upper = ((rank_ref[0] >> level) & 1) == 1
        dot_value, norm_mine, norm_theirs = [jnp.sum(t, axis=0, keepdims=True) for t in totals]
        out[...] = jnp.zeros_like(out) if before is None else refs[-2][...]
        base = 3 * layer
        out[base : base + 1, :] = dot_value
        out[base + 1 : base + 2, :] = jnp.where(upper, norm_theirs, norm_mine)
        out[base + 2 : base + 3, :] = jnp.where(upper, norm_mine, norm_theirs)

    shape = jax.ShapeDtypeStruct((-(-3 * layers // 8) * 8, LANES), jnp.float32)
    inputs = list(kept) + [part for parts in received for part in parts]
    inputs += [] if before is None else [before]
    return call(kernel, "pair_rows", rank, inputs, [shape])[0]


def pair_combine(rank, sums, kept, received, level):
    layers, count = len(kept), len(kept[0])
    ways = len(received[0][0])
    rows, width = kept[0][0].shape

    def kernel(rank_ref, sums_ref, *refs):
        ins, outs = refs[:-count], refs[-count:]
        totals = jnp.sum(sums_ref[...], axis=1, keepdims=True)
        upper = ((rank_ref[0] >> level) & 1) == 1
        for layer in range(layers):
            dot_value, norm_first, norm_second = [
                totals[3 * layer + k : 3 * layer + k + 1] for k in range(3)
            ]
            first, second = scale_pair(dot_value, norm_first, norm_second)
            mine = jnp.broadcast_to(jnp.where(upper, second, first), (STRIDE, LANES))
            theirs = jnp.broadcast_to(jnp.where(upper, first, second), (STRIDE, LANES))
            for number in range(count):
                left, *others = ins[(1 + ways) * (layer * count + number) :][: 1 + ways]
                out = outs[number]

                def step(where, columns, carry, left=left, others=others, out=out):
                    right = chosen_rows(rank_ref, level, others, where, columns)
                    out[layer, where, columns] = weighted(mine, left[where, columns], theirs, right)
                    return carry

                tiles(rows, width, step, 0)

    shape = jax.ShapeDtypeStruct((layers, rows, width), jnp.bfloat16)
    inputs = [sums]
    for layer in range(layers):
        for left, others in zip(kept[layer], received[layer]):
            inputs += [left] + list(others)
    return call(kernel, "pair_combine", rank, inputs, [shape] * count)


def level_masks(levels):
    masks = [1 << level for level in range(levels)]
    if levels >= 3:
        masks[-1] |= masks[-2]
    return masks


def spread(code, masks):
    value = 0
    for bit, mask in enumerate(masks):
        if code >> bit & 1:
            value ^= mask
    return value


def swap(value, mask, middle=None):
    pairs = [(i, i ^ mask) for i in range(lax.axis_size("rep"))]
    if middle is not None:
        high = mask.bit_length() - 1
        pairs = [(i, j) for i, j in pairs if ((i >> high & 1) != (i >> (high - 1) & 1)) == middle]
    return lax.ppermute(value, "rep", pairs)


def body(activations, output_grads):
    replicas = lax.axis_size("rep")
    par = lax.axis_size("par")
    levels = replicas.bit_length() - 1
    layers, tokens, width = activations.shape
    rows = width // replicas
    rank = lax.axis_index("rep")
    position = jnp.reshape(rank, (1,)).astype(jnp.int32)
    masks = level_masks(levels)
    tails = [tail << 2 for tail in reversed(range(replicas // GROUP))]

    own, crossed, far, far_crossed = {}, {}, {}, {}
    rounds = []
    for layer in range(layers):
        codes = [2 | tail for tail in tails] + tails
        second = [(own, far, 2 | tail) for tail in tails]
        second += [(crossed, far_crossed, 2 | tail) for tail in tails]
        rounds += [(layer, code) + unit for code, unit in zip(codes, second)]
    window = 2

    def settle(number, sends):
        layer, code, _, target, block = rounds[number]
        key, other = (layer, code), (layer, block ^ 2)
        sends, (crossed[key], target[other]) = tied(sends, [crossed[key], target[other]])
        return sends

    spans = []
    stride = 1
    while stride < par:
        spans.append([("par", stride)])
        stride *= 2

    def summed(value, hops):
        for hop in hops:
            if len(hop) == 2 and MESH_HOPS:
                first, second = hop
                both = {}
                for axis, mask in hop:
                    both[axis] = both.get(axis, 0) ^ mask
                parts = [value] + [exchange(value, *one) for one in hop] + [exchange_all(value, both)]
                value = total(parts, COST)
            else:
                for axis, mask in hop:
                    value = value + exchange(value, axis, mask)
        return value

    def layer_gram(layer):
        gram = None
        for tail in tails:
            parts = [held[layer, tail] for held in (own, crossed, far, far_crossed)]
            cost = COST if layer < layers - 1 else FIRST_COST if gram is None else GRAM_COST
            gram = gram_rows(position, parts, gram, cost)
        return gram

    def group_result(layer, gram):
        parts = [
            [held[layer, tail] for held in (own, crossed, far, far_crossed)] for tail in tails
        ]
        return {
            tail: group_combine(
                position, gram, [block_parts], KEPT_COST if layer == layers - 1 and tail == 0 else COST
            )[0]
            for tail, block_parts in zip(tails, parts)
        }

    def receive(blocks, level, middle):
        mask = masks[level]
        sends = [blocks[tail | 1 << level] for tail in blocks if not tail >> level & 1]
        if mask == 1 << level:
            return [[swap(sent, mask)] if middle else [] for sent in sends]
        return [[swap(sent, mask, middle)] for sent in sends]

    def receive_all(blocks, level):
        return [a + b for a, b in zip(receive(blocks, level, True), receive(blocks, level, False))]

    def tied_ways(values, ways):
        flat = [part for way in ways for part in way]
        values, flat = tied(values, flat)
        return values, [[flat.pop(0) for _ in way] for way in ways]

    inputs = activations
    per_layer = len(rounds) // layers
    combined, received, sends = [], [], {}

    def multiply(number):
        nonlocal inputs
        if number >= 2 * window:
            (inputs,) = settle(number - 2 * window, [inputs])
        layer = rounds[number][0]
        batch = [number]
        while (batch[-1] + 1) % per_layer and (batch[-1] + 1) % per_layer not in BATCHES[layer > 0]:
            batch.append(batch[-1] + 1)
        offsets = [spread(rounds[index][1], masks) for index in batch]
        values = block_pairs(position, inputs, output_grads, layer, offsets, rows)
        for index, (kept, sent) in zip(batch, values):
            own[layer, rounds[index][1]], sends[index] = kept, sent

    for number in range(len(rounds)):
        layer, code, source, target, block = rounds[number]
        if number not in sends:
            multiply(number)
        sent, passed = sends[number], source[layer, block]
        done, step = divmod(number - window + 1, per_layer)
        if number >= window:
            sent, passed = settle(number - window, [sent, passed])
        if done >= 1 and step == 1:
            (sent, passed), (gram,) = tied([sent, passed], [layer_gram(done - 1)])
            parts = [gram] + [exchange(gram, "rep", mask) for mask in range(1, GROUP)]
            combined.append(group_result(done - 1, summed(total(parts, CROSS_COST), spans)))
            received.append(receive(combined[-1], 2, True))
        crossed[layer, code] = exchange(sent, "rep", masks[0])
        target[layer, block ^ 2] = exchange(passed, "rep", masks[1])

    first = (layers - 1, tails[0])
    for layer in range(layers - 1):
        names = list(combined[layer])
        values = [combined[layer][tail] for tail in names]
        values, (own[first],) = tied(values, [own[first]])
        combined[layer] = dict(zip(names, values))
    gram = summed(layer_gram(layers - 1), [[("rep", masks[1])]])
    for layer in range(layers - 1):
        names = list(combined[layer])
        values, (gram,) = tied([combined[layer][tail] for tail in names], [gram])
        combined[layer] = dict(zip(names, values))
        outer = receive(combined[layer], 2, False)
        gram = summed(gram, spans[:1])
        (gram,), received[layer] = tied_ways([gram], received[layer])
        received[layer] = [a + b for a, b in zip(received[layer], outer)]
    gram = summed(gram, spans[1:-1] + [spans[-1] + [("rep", masks[0])]])
    combined.append(group_result(layers - 1, gram))
    names = [tail for tail in tails if tail >> 2 & 1]
    values = [combined[-1][tail] for tail in names]
    for layer in range(layers - 1):
        inner = [way[:1] for way in received[layer]]
        values, inner = tied_ways(values, inner)
        received[layer] = [a + b[1:] for a, b in zip(inner, received[layer])]
    combined[-1].update(zip(names, values))
    received.append(receive_all(combined[-1], 2))

    for level in range(2, levels):
        keep = [tail for tail in tails if not tail >> level & 1 and tail in combined[0]]
        kept = [[combined[layer][tail] for tail in keep] for layer in range(layers)]
        totals = None
        for layer in range(layers):
            totals = pair_rows(position, kept[layer], received[layer], level, layer, layers, totals)
        bits = [("rep", 1 << bit) for bit in range(level + 1)]
        hops = spans[:-1] + [spans[-1] + bits[:1]] + [bits[i : i + 2] for i in range(1, level + 1, 2)]
        totals = summed(totals, hops)
        results = pair_combine(position, totals, kept, received, level)
        if level < levels - 1:
            combined = [
                {tail: result[layer] for tail, result in zip(keep, results)} for layer in range(layers)
            ]
            received = [receive_all(combined[layer], level + 1) for layer in range(layers)]
    return results[0]


def solution(mesh):
    return jax.shard_map(
        body,
        mesh=mesh,
        in_specs=(P(None, "rep", "par"), P(None, "rep", None)),
        out_specs=P(None, ("par", "rep"), None),
        check_vma=False,
    )
```
